256 devices in a mesh: row: 32 (over z_hi, y, core), chan: 8 (over z_lo, x).
Axes of the slice: x: 4, y: 4, z: 8 (z_hi: 4, z_lo: 2; z = z_hi * 2 + z_lo), core: 2. Of those that a mesh axis runs over, the one named last changes fastest.
Arguments:
- pair_input: bfloat16 [768, 768, 128], P('row', 'chan'), may hold values from -6 to 6
- token_valid: int32 [768], replicated, may hold values from 0 to 1, as said below
- left_proj: bfloat16 [128, 128], replicated, may hold values from -0.5 to 0.5
- left_gate: bfloat16 [128, 128], replicated, may hold values from -0.5 to 0.5
- right_proj: bfloat16 [128, 128], replicated, may hold values from -0.5 to 0.5
- right_gate: bfloat16 [128, 128], replicated, may hold values from -0.5 to 0.5
- mult_gate: bfloat16 [128, 128], replicated, may hold values from -0.5 to 0.5
- mult_out: bfloat16 [128, 128], replicated, may hold values from -1 to 1
- query_weight: bfloat16 [128, 128], replicated, may hold values from -0.5 to 0.5
- key_weight: bfloat16 [128, 128], replicated, may hold values from -0.5 to 0.5
- value_weight: bfloat16 [128, 128], replicated, may hold values from -0.5 to 0.5
- bias_weight: bfloat16 [128, 4], replicated, may hold values from -64 to 64
- heads_gate: bfloat16 [128, 128], replicated, may hold values from -0.5 to 0.5
- heads_out: bfloat16 [128, 128], replicated, may hold values from -2 to 2
- swish_in: bfloat16 [128, 512], replicated, may hold values from -0.5 to 0.5
- linear_in: bfloat16 [128, 512], replicated, may hold values from -0.5 to 0.5
- project_out: bfloat16 [512, 128], replicated, may hold values from -0.25 to 0.25
Outputs:
- pair_output: bfloat16 [768, 768, 128], P('row', 'chan')
The draws below stay inside these ranges and needn't reach their ends.
Inputs may be any that keep to these rules, and one draw needn't show every extreme that they name: `token_valid`: 1 marks a real token and 0 padding. The crop holds four chains of 192 tokens each, every chain real up to some point and padded after it, with at least half of each chain real.
All inputs are finite; a program needn't handle non-finite values.
Results may differ from the reference program's by a relative error of at most 0.034.
The reference program's roundings to bfloat16 on the way count: a program that leaves them out, or rounds other values in their place, can miss the bound.
Values may be sent and summed in bfloat16 or wider, within the bound.
A program may use at most 128 MiB of HBM per device.

```python
import math
import jax
import jax.numpy as jnp
from jax import lax

C = 128
C_TRI = 128
H = 4
DH = 32
TRANS = 512
CROP = 768


def draw_token_valid(key, part):
    key = jax.random.fold_in(key, 5)
    crop_size = CROP
    span_length = crop_size // 4
    chain_ends = jax.random.randint(key, (4,), span_length // 2, span_length)
    position = jnp.arange(crop_size)
    chain_index = position // span_length
    return (position % span_length < chain_ends[chain_index]).astype(jnp.int32)


def draw_bias_weight(key, part):
    key = jax.random.fold_in(key, 11)
    base_values = jax.random.normal(key, (C, H), jnp.float32)
    head_scale = 1.5 * jnp.ones((H,), jnp.float32)
    return (base_values * head_scale[None, :] / math.sqrt(C)).astype(jnp.bfloat16)


def levels(stream_key, dims, shards, smallest, high):
    def one(dim, blocks):
        draws = jax.random.uniform(jax.random.fold_in(jax.random.fold_in(stream_key, 6), dim), (blocks,), jnp.float32, smallest / len(shards), high / len(shards))
        return jnp.repeat(jnp.exp(draws), dims[dim] // blocks).reshape((-1,) + (1,) * (len(dims) - dim - 1))

    factor_of = one(*shards[0])
    for cut in shards[1:]:
        factor_of = factor_of * one(*cut)
    return factor_of


def normal_values(own_key, shape, deviation, bound, pieces=(), held_as=jnp.bfloat16):
    values = deviation * jax.random.normal(own_key, shape, jnp.float32)
    if pieces:
        values = values * levels(own_key, shape, pieces, -0.22, 0.18)
    return jnp.clip(values, -bound, bound).astype(held_as)


def setup_inputs(seed: int = 0) -> dict:
    arg_keys = jax.random.split(jax.random.key(seed), 18)
    pair_input = normal_values(arg_keys[0], (CROP, CROP, C), 1.0, 6.0, ((0, 32), (1, 8)))
    token_valid = draw_token_valid(jax.random.fold_in(arg_keys[17], 71), 0)
    left_proj = normal_values(arg_keys[2], (C, C_TRI), C ** -0.5, 0.5)
    left_gate = normal_values(arg_keys[3], (C, C_TRI), C ** -0.5, 0.5)
    right_proj = normal_values(arg_keys[4], (C, C_TRI), C ** -0.5, 0.5)
    right_gate = normal_values(arg_keys[5], (C, C_TRI), C ** -0.5, 0.5)
    mult_gate = normal_values(arg_keys[6], (C, C), C ** -0.5, 0.5)
    mult_out = normal_values(arg_keys[7], (C_TRI, C), (C_TRI // 4) ** -0.5, 1.0)
    query_weight = normal_values(arg_keys[8], (C, H * DH), C ** -0.5, 0.5)
    key_weight = normal_values(arg_keys[9], (C, H * DH), C ** -0.5, 0.5)
    value_weight = normal_values(arg_keys[10], (C, H * DH), C ** -0.5, 0.5)
    bias_weight = draw_bias_weight(jax.random.fold_in(arg_keys[17], 71), 0)
    heads_gate = normal_values(arg_keys[12], (C, H * DH), C ** -0.5, 0.5)
    heads_out = normal_values(arg_keys[13], (H * DH, C), (H * DH // 16) ** -0.5, 2.0)
    swish_in = normal_values(arg_keys[14], (C, TRANS), C ** -0.5, 0.5)
    linear_in = normal_values(arg_keys[15], (C, TRANS), C ** -0.5, 0.5)
    project_out = normal_values(arg_keys[16], (TRANS, C), TRANS ** -0.5, 0.25)
    return {"pair_input": pair_input, "token_valid": token_valid, "left_proj": left_proj, "left_gate": left_gate, "right_proj": right_proj, "right_gate": right_gate, "mult_gate": mult_gate, "mult_out": mult_out, "query_weight": query_weight, "key_weight": key_weight, "value_weight": value_weight, "bias_weight": bias_weight, "heads_gate": heads_gate, "heads_out": heads_out, "swish_in": swish_in, "linear_in": linear_in, "project_out": project_out}


def layer_norm(values, dimension):
    values = values.astype(jnp.float32)
    center = lax.optimization_barrier(jnp.mean(values, axis=dimension, keepdims=True))
    spread = lax.optimization_barrier(jnp.mean(jnp.square(values - center), axis=dimension, keepdims=True))
    return (values - center) * lax.rsqrt(spread + 1e-05)

def project(inputs, matrix):
    return jnp.einsum('ijc,cd->ijd', inputs.astype(jnp.float32), matrix.astype(jnp.float32))

def reference(pair_input, token_valid, left_proj, left_gate, right_proj, right_gate, mult_gate, mult_out, query_weight, key_weight, value_weight, bias_weight, heads_gate, heads_out, swish_in, linear_in, project_out):
    crop_size = pair_input.shape[0]
    validity = token_valid.astype(jnp.float32)
    pair_mask = (validity[:, None] * validity[None, :])[:, :, None]
    normed = layer_norm(pair_input, 2).astype(jnp.bfloat16)
    left_side = (pair_mask * jax.nn.sigmoid(project(normed, left_gate)) * project(normed, left_proj)).astype(jnp.bfloat16)
    right_side = (pair_mask * jax.nn.sigmoid(project(normed, right_gate)) * project(normed, right_proj)).astype(jnp.bfloat16)
    product = jnp.einsum('ikc,jkc->ijc', left_side.astype(jnp.float32), right_side.astype(jnp.float32))
    product_norm = layer_norm(product, 2).astype(jnp.bfloat16)
    update = jax.nn.sigmoid(project(normed, mult_gate)) * project(product_norm, mult_out)
    after_mult = (pair_input.astype(jnp.float32) + update).astype(jnp.bfloat16)
    normed = layer_norm(after_mult, 2).astype(jnp.bfloat16)
    queries = project(normed, query_weight).astype(jnp.bfloat16).reshape(crop_size, crop_size, H, DH)
    keys_all = project(normed, key_weight).astype(jnp.bfloat16).reshape(crop_size, crop_size, H, DH)
    values_all = project(normed, value_weight).astype(jnp.bfloat16).reshape(crop_size, crop_size, H, DH)
    gate_value = jax.nn.sigmoid(project(normed, heads_gate))
    bias_table = jnp.einsum('jkc,ch->hjk', normed.astype(jnp.float32), bias_weight.astype(jnp.float32))
    key_alive = validity > 0.5

    def one_row(operands):
        query_row, key_row, value_row = operands
        score = jnp.einsum('jhd,khd->hjk', query_row.astype(jnp.float32), key_row.astype(jnp.float32)) / math.sqrt(DH) + bias_table
        score = jnp.where(key_alive[None, None, :], score, -1e+30)
        row_peak = lax.optimization_barrier(jnp.max(score, axis=2, keepdims=True))
        raised = jnp.exp(score - row_peak)
        weights = raised.astype(jnp.bfloat16)
        summed = jnp.einsum('hjk,khd->jhd', weights.astype(jnp.float32), value_row.astype(jnp.float32))
        return summed / jnp.transpose(lax.optimization_barrier(jnp.sum(raised, axis=2)))[:, :, None]
    attended = lax.map(one_row, (queries, keys_all, values_all)).reshape(crop_size, crop_size, H * DH)
    heads = (gate_value * attended).astype(jnp.bfloat16)
    second = (after_mult.astype(jnp.float32) + project(heads, heads_out)).astype(jnp.bfloat16)

    def transition_row(row_values):
        normed_row = layer_norm(row_values, 1).astype(jnp.bfloat16).astype(jnp.float32)
        gated = jnp.dot(normed_row, swish_in.astype(jnp.float32))
        linear = jnp.dot(normed_row, linear_in.astype(jnp.float32))
        hidden = (jax.nn.silu(gated) * linear).astype(jnp.bfloat16)
        down = jnp.dot(hidden.astype(jnp.float32), project_out.astype(jnp.float32))
        return (row_values.astype(jnp.float32) + down).astype(jnp.bfloat16)
    return lax.map(transition_row, second)
```

```python
import math

import jax
import jax.numpy as jnp
from jax import lax
from jax.experimental import pallas as pl
from jax.experimental.pallas import tpu as pltpu
from jax.sharding import PartitionSpec as P

BF16 = jnp.bfloat16
F32 = jnp.float32
LOG2E = math.log2(math.e)
MESH = pl.DeviceIdType.MESH
VMEM = pl.BlockSpec(memory_space=pltpu.VMEM)
ANY = pl.BlockSpec(memory_space=pl.ANY)
LIMIT = 60 * 1024 * 1024


def normalize(values, axis):
    center = jnp.mean(values, axis=axis, keepdims=True)
    spread = jnp.mean(jnp.square(values - center), axis=axis, keepdims=True)
    return (values - center) * lax.rsqrt(spread + 1e-05)


def dot(a, b, a_dim=1, b_dim=0):
    return lax.dot_general(a, b, (((a_dim,), (b_dim,)), ((), ())), preferred_element_type=F32)


def transposed(ref):
    return ref[...].astype(F32).T.astype(BF16)


def remote(src, dst, send_sem, recv_sem, row, chan):
    return pltpu.make_async_remote_copy(
        src_ref=src,
        dst_ref=dst,
        send_sem=send_sem,
        recv_sem=recv_sem,
        device_id=(row, chan),
        device_id_type=MESH,
    )


def triangle_kernel(
    pair_ref,
    mask_ref,
    left_proj_ref,
    left_gate_ref,
    right_proj_ref,
    right_gate_ref,
    mult_gate_ref,
    mult_out_ref,
    bias_weight_ref,
    after_ref,
    normed_ref,
    bias_ref,
    left_f,
    right_f,
    send,
    mine,
    theirs,
    left_all,
    right_all,
    product,
    back,
    gate_f,
    norm_f,
    bias_f,
    send_sem,
    recv_sem,
    local_sem,
):
    rows, columns, channels = pair_ref.shape
    chips_down, chips_across = product.shape[0], product.shape[1]
    chips = chips_down * chips_across
    row, chan = lax.axis_index("row"), lax.axis_index("chan")
    core, down = row % 2, row // 2
    here = down * chips_across + chan

    weights = jnp.concatenate(
        [transposed(ref) for ref in (left_gate_ref, left_proj_ref, right_gate_ref, right_proj_ref)],
        axis=0,
    )
    pad = jnp.zeros((128 - columns, channels), BF16)

    def edges(i, carry):
        normed = normalize(pair_ref[i].astype(F32), 1).astype(BF16)
        out = dot(weights, jnp.concatenate([normed, pad], axis=0), 1, 1)
        mask = mask_ref[i]
        at = pl.ds(pl.multiple_of(i * channels, channels), channels)
        left_f[at, :] = mask * jax.nn.sigmoid(out[0:128]) * out[128:256]
        right_f[at, :] = mask * jax.nn.sigmoid(out[256:384]) * out[384:512]
        return carry

    lax.fori_loop(0, rows, edges, 0)

    def regroup(channel, carry):
        at = pl.ds(channel, rows, stride=channels)
        send[channel] = jnp.concatenate([right_f[at, :], left_f[at, :]], axis=0).astype(BF16)
        return carry

    lax.fori_loop(0, channels, regroup, 0)

    def out_copy(step):
        other = (here + step * 37) % chips
        down_to, chan_to = other // chips_across, other % chips_across
        return remote(
            send.at[other],
            mine.at[here],
            send_sem.at[0],
            recv_sem.at[0],
            down_to * 2 + core,
            chan_to,
        )

    lax.fori_loop(1, chips, lambda step, carry: (out_copy(step).start(), carry)[1], 0)
    own = pltpu.make_async_copy(send.at[here], mine.at[here], local_sem.at[0])
    own.start()

    def gates(i, carry):
        normed = normalize(pair_ref[i].astype(F32), 1).astype(BF16)
        gate_f[i] = jax.nn.sigmoid(dot(normed, mult_gate_ref[...]))
        return carry

    lax.fori_loop(0, rows, gates, 0)
    own.wait()
    arrived = mine.at[pl.ds(0, chips - 1)]
    pltpu.make_async_copy(arrived, arrived, recv_sem.at[0]).wait()
    sent = send.at[pl.ds(0, chips - 1)]
    pltpu.make_async_copy(sent, sent, send_sem.at[0]).wait()

    swap = remote(
        mine.at[:, pl.ds(0, 32), :], theirs, send_sem.at[1], recv_sem.at[1], row + 1 - 2 * core, chan
    )
    swap.start()
    for c in range(chips_across):
        lanes = pl.ds(c * 128, 128)
        for d in range(chips_down):
            left_all[pl.ds(d * 32, 32), lanes] = mine[d * chips_across + c, 16:48, :]
            right_all[d, core, :, lanes] = mine[d * chips_across + c, 0:32, :]
    swap.wait()
    for c in range(chips_across):
        lanes = pl.ds(c * 128, 128)
        for d in range(chips_down):
            right_all[d, 1 - core, :, lanes] = theirs[d * chips_across + c]
    width = 128 * chips_across
    for c in range(0, chips_across, 2):
        right = right_all[c * 2 : c * 2 + 4].reshape(256, width)
        out = dot(left_all[...], right, 1, 1).astype(BF16)
        product[:, c] = out[:, 0:128].reshape(chips_down, 32, 128)
        product[:, c + 1] = out[:, 128:256].reshape(chips_down, 32, 128)

    def back_copy(step):
        other = (here + step * 37) % chips
        down_to, chan_to = other // chips_across, other % chips_across
        return remote(
            product.at[down_to, chan_to],
            back.at[here],
            send_sem.at[2],
            recv_sem.at[2],
            down_to * 2 + core,
            chan_to,
        )

    lax.fori_loop(1, chips, lambda step, carry: (back_copy(step).start(), carry)[1], 0)
    own = pltpu.make_async_copy(product.at[down, chan], back.at[here], local_sem.at[0])
    own.start()
    own.wait()
    arrived = back.at[pl.ds(0, chips - 1)]
    pltpu.make_async_copy(arrived, arrived, recv_sem.at[2]).wait()
    pltpu.make_async_copy(arrived, arrived, send_sem.at[2]).wait()

    def total(channel, carry):
        return carry + back[channel].astype(F32)[8:32]

    zero = jnp.zeros((rows, 128), F32)
    center = lax.fori_loop(0, channels, total, zero, unroll=8) * (1.0 / channels)

    def square(channel, carry):
        return carry + jnp.square(back[channel].astype(F32)[8:32] - center)

    spread = lax.fori_loop(0, channels, square, zero, unroll=8) * (1.0 / channels)
    scale = lax.rsqrt(spread + 1e-05)

    def scaled(channel, carry):
        at = pl.ds(pl.multiple_of(channel * rows, 8), rows)
        norm_f[at, :] = (back[channel].astype(F32)[8:32] - center) * scale
        return carry

    lax.fori_loop(0, channels, scaled, 0, unroll=8)
    bias_weights = bias_weight_ref[...].astype(F32).T.astype(BF16)
    heads = bias_weights.shape[0]
    bias_weights = jnp.concatenate(
        [bias_weights.astype(F32), jnp.zeros((8 - heads, channels), F32)], axis=0
    ).astype(BF16)

    def finish(i, carry):
        product_norm = norm_f[pl.ds(i, channels, stride=rows), :].astype(BF16)
        out = dot(product_norm, mult_out_ref[...], 0, 0)
        out = jnp.concatenate([out[32 * k : 32 * k + rows] for k in range(4)], axis=0)
        after = (pair_ref[i].astype(F32) + gate_f[i] * out).astype(BF16)
        after_ref[i] = after
        normed = normalize(after.astype(F32), 1).astype(BF16)
        normed_ref[i] = normed
        at = pl.ds(pl.multiple_of(i * 8, 8), 8)
        bias_f[at, :] = dot(bias_weights, jnp.concatenate([normed, pad], axis=0), 1, 1)
        return carry

    lax.fori_loop(0, rows, finish, 0)
    for h in range(heads):
        bias_ref[h] = bias_f[pl.ds(h, rows, stride=8), :]


def gather_kernel(
    normed_ref, bias_ref, all_ref, mine_ref, theirs_ref, send_sem, recv_sem, local_sem, bias_sem
):
    row, chan = lax.axis_index("row"), lax.axis_index("chan")
    core, down = row % 2, row // 2
    downs = 16
    zone, place = chan // 4, chan % 4
    right, left = (place + 1) % 4, (place + 3) % 4
    half = normed_ref.shape[0] // 2

    def block(z, x):
        return all_ref.at[z * 4 + x]

    def first(ref):
        return ref.at[pl.ds(0, half)]

    def second(ref):
        return ref.at[pl.ds(half, half)]

    def copy(slot, src, dst, z, x):
        return remote(src, dst, send_sem.at[slot], recv_sem.at[slot], row, z * 4 + x)

    own = pltpu.make_async_copy(normed_ref, all_ref.at[chan], local_sem.at[0])
    own.start()
    here = block(zone, place)
    copies = {}

    def go(slot, src, dst, z, x):
        copies[slot] = copy(slot, src, dst, z, x)
        copies[slot].start()

    go(0, normed_ref, here, 1 - zone, place)
    go(1, normed_ref, here, zone, right)
    go(2, normed_ref, here, zone, left)

    column = row // 4
    part = (row % 4) // 2
    landing = mine_ref.at[part, chan]
    for d in range(downs):
        self_copy = jnp.logical_and(down == d, chan == column)

        @pl.when(self_copy)
        def _():
            pltpu.make_async_copy(bias_ref, landing, bias_sem.at[1]).start()

        @pl.when(jnp.logical_not(self_copy))
        def _():
            remote(bias_ref, landing, bias_sem.at[0], bias_sem.at[1], d * 2 + core, column).start()

    copies[0].wait_recv()
    across = block(1 - zone, place)
    go(3, across, across, zone, right)
    go(4, across, across, zone, left)
    copies[1].wait_recv()
    from_left = first(block(zone, left))
    go(5, from_left, from_left, zone, right)
    copies[2].wait_recv()
    from_right = second(block(zone, right))
    go(6, from_right, from_right, zone, left)

    pltpu.make_async_copy(mine_ref, mine_ref, bias_sem.at[1]).wait()
    swap = remote(
        mine_ref, theirs_ref, bias_sem.at[2], bias_sem.at[3], row + 1 - 2 * core, chan
    )
    swap.start()

    copies[3].wait_recv()
    from_left = first(block(1 - zone, left))
    go(7, from_left, from_left, zone, right)
    copies[4].wait_recv()
    from_right = second(block(1 - zone, right))
    go(8, from_right, from_right, zone, left)
    for slot in (5, 6, 7, 8):
        copies[slot].wait_recv()
    for slot in range(9):
        copies[slot].wait_send()
    own.wait()
    swap.wait()
    for d in range(downs):
        self_copy = jnp.logical_and(down == d, chan == column)

        @pl.when(jnp.logical_not(self_copy))
        def _():
            remote(
                bias_ref, landing, bias_sem.at[0], bias_sem.at[1], d * 2 + core, column
            ).wait_send()


def attention_kernel(
    core_ref,
    all_ref,
    own_ref,
    after_ref,
    mine_ref,
    theirs_ref,
    alive_ref,
    query_ref,
    key_ref,
    value_ref,
    gate_ref,
    heads_out_ref,
    swish_ref,
    linear_ref,
    project_ref,
    out_ref,
    bias_f,
    attended_f,
):
    blocks, step_rows, columns, channels = all_ref.shape
    heads, parts, part_rows, keys = bias_f.shape
    queries = parts * part_rows
    core = core_ref[0]

    @pl.when(pl.program_id(0) == 0)
    def _():
        alive = alive_ref[...] > 0.5
        for h in range(heads):
            for part in range(2):
                for ref, side in ((mine_ref, core), (theirs_ref, 1 - core)):
                    line = jnp.concatenate(
                        [ref[part, c, h][:, 0:columns] for c in range(blocks)], axis=1
                    )
                    bias_f[h, 2 * part + side] = jnp.where(alive, line * LOG2E, -1e30)

    head_of_lane = lax.broadcasted_iota(jnp.int32, (queries, channels), 1) // (channels // heads)
    scale = LOG2E / math.sqrt(channels // heads)
    key_value = jnp.concatenate([key_ref[...], value_ref[...]], axis=1)
    ones = jnp.ones((keys, channels), BF16)

    for t in range(step_rows):
        tokens = jnp.concatenate([all_ref[c, t] for c in range(blocks)], axis=0)
        projected = dot(tokens, key_value).astype(BF16)
        key, value = projected[:, 0:channels], projected[:, channels:]
        query = dot(own_ref[t], query_ref[...])
        spread = jnp.concatenate(
            [jnp.where(head_of_lane == h, query, 0.0) for h in range(heads)], axis=0
        ).astype(BF16)
        score = dot(spread, key, 1, 1) * scale + bias_f[...].reshape(heads * queries, keys)
        raised = jnp.exp2(score - jnp.max(score, axis=1, keepdims=True)).astype(BF16)
        summed = dot(raised, jnp.concatenate([value, ones], axis=1))
        top = jnp.zeros((queries, channels), F32)
        bottom = jnp.zeros((queries, channels), F32)
        for h in range(heads):
            at = slice(h * queries, (h + 1) * queries)
            top = jnp.where(head_of_lane == h, summed[at, 0:channels], top)
            bottom = jnp.where(head_of_lane == h, summed[at, channels:], bottom)
        attended_f[pl.ds(t * queries, queries), :] = top / bottom

    normed = own_ref[...].reshape(step_rows * columns, channels)
    gate = jax.nn.sigmoid(dot(normed, gate_ref[...]))
    mixed = (gate * attended_f[...]).astype(BF16)
    after = after_ref[...].reshape(step_rows * columns, channels).astype(F32)
    second = (after + dot(mixed, heads_out_ref[...])).astype(BF16)
    second_f = second.astype(F32)
    normed = normalize(second_f, 1).astype(BF16)
    hidden = (jax.nn.silu(dot(normed, swish_ref[...])) * dot(normed, linear_ref[...])).astype(BF16)
    out = (second_f + dot(hidden, project_ref[...])).astype(BF16)
    out_ref[...] = out.reshape(step_rows, columns, channels)


def body(
    pair_input,
    token_valid,
    left_proj,
    left_gate,
    right_proj,
    right_gate,
    mult_gate,
    mult_out,
    query_weight,
    key_weight,
    value_weight,
    bias_weight,
    heads_gate,
    heads_out,
    swish_in,
    linear_in,
    project_out,
):
    rows, columns, channels = pair_input.shape
    heads = bias_weight.shape[1]
    tokens = token_valid.shape[0]
    across = tokens // columns
    down = tokens // rows // 2
    chips = across * down
    row, chan = lax.axis_index("row"), lax.axis_index("chan")
    validity = token_valid.astype(F32)
    row_valid = lax.dynamic_slice_in_dim(validity, row * rows, rows)
    column_valid = lax.dynamic_slice_in_dim(validity, chan * columns, columns)
    column_valid = jnp.pad(column_valid, (0, 128 - columns))
    mask = (row_valid[:, None] * column_valid[None, :]).reshape(rows, 1, 128)

    after, normed, bias = pl.pallas_call(
        triangle_kernel,
        out_shape=[
            jax.ShapeDtypeStruct((rows, columns, channels), BF16),
            jax.ShapeDtypeStruct((rows, columns, channels), BF16),
            jax.ShapeDtypeStruct((heads, rows, 128), F32),
        ],
        in_specs=[VMEM] * 9,
        out_specs=[VMEM] * 3,
        scratch_shapes=[
            pltpu.VMEM((rows * channels, 128), F32),
            pltpu.VMEM((rows * channels, 128), F32),
            pltpu.VMEM((chips, 48, 128), BF16),
            pltpu.VMEM((chips, 48, 128), BF16),
            pltpu.VMEM((chips, 32, 128), BF16),
            pltpu.VMEM((down * 32, across * 128), BF16),
            pltpu.VMEM((down, 2, 32, across * 128), BF16),
            pltpu.VMEM((down, across, 32, 128), BF16),
            pltpu.VMEM((chips, 32, 128), BF16),
            pltpu.VMEM((rows, columns, channels), F32),
            pltpu.VMEM((channels * rows, 128), F32),
            pltpu.VMEM((rows * 8, 128), F32),
            pltpu.SemaphoreType.DMA((3,)),
            pltpu.SemaphoreType.DMA((3,)),
            pltpu.SemaphoreType.DMA((1,)),
        ],
        compiler_params=pltpu.CompilerParams(has_side_effects=True, vmem_limit_bytes=LIMIT),
        name="triangle",
    )(
        pair_input,
        mask,
        left_proj,
        left_gate,
        right_proj,
        right_gate,
        mult_gate,
        mult_out,
        bias_weight,
    )

    everything, bias_mine, bias_theirs = pl.pallas_call(
        gather_kernel,
        out_shape=[
            jax.ShapeDtypeStruct((across, rows, columns, channels), BF16),
            jax.ShapeDtypeStruct((2, across, heads, rows, 128), F32),
            jax.ShapeDtypeStruct((2, across, heads, rows, 128), F32),
        ],
        in_specs=[ANY] * 2,
        out_specs=[ANY] * 3,
        scratch_shapes=[
            pltpu.SemaphoreType.DMA((9,)),
            pltpu.SemaphoreType.DMA((9,)),
            pltpu.SemaphoreType.DMA((1,)),
            pltpu.SemaphoreType.DMA((4,)),
        ],
        compiler_params=pltpu.CompilerParams(has_side_effects=True),
        name="gather",
    )(normed, bias)

    step_rows = 4
    block = pl.BlockSpec((step_rows, columns, channels), lambda i: (i, 0, 0))
    return pl.pallas_call(
        attention_kernel,
        out_shape=jax.ShapeDtypeStruct((rows, columns, channels), BF16),
        grid=(rows // step_rows,),
        in_specs=[
            pl.BlockSpec(memory_space=pltpu.SMEM),
            pl.BlockSpec((across, step_rows, columns, channels), lambda i: (0, i, 0, 0)),
            block,
            block,
        ]
        + [VMEM] * 11,
        out_specs=block,
        scratch_shapes=[
            pltpu.VMEM((heads, 4, rows, tokens), F32),
            pltpu.VMEM((step_rows * columns, channels), F32),
        ],
        compiler_params=pltpu.CompilerParams(vmem_limit_bytes=LIMIT),
        name="attention",
    )(
        (row % 2).reshape(1).astype(jnp.int32),
        everything,
        normed,
        after,
        bias_mine,
        bias_theirs,
        validity.reshape(1, tokens),
        query_weight,
        key_weight,
        value_weight,
        heads_gate,
        heads_out,
        swish_in,
        linear_in,
        project_out,
    )


def solution(mesh):
    return jax.shard_map(
        body,
        mesh=mesh,
        in_specs=(P("row", "chan", None),) + (P(),) * 16,
        out_specs=P("row", "chan", None),
        check_vma=False,
    )
```

```python
import math

import jax
import jax.numpy as jnp
from jax import lax
from jax.experimental import pallas as pl
from jax.experimental.pallas import tpu as pltpu
from jax.sharding import PartitionSpec as P

BF16 = jnp.bfloat16
F32 = jnp.float32
LOG2E = math.log2(math.e)
MESH = pl.DeviceIdType.MESH
VMEM = pl.BlockSpec(memory_space=pltpu.VMEM)
LIMIT = 60 * 1024 * 1024
GROUP = 4


def normalize(values, axis):
    center = jnp.mean(values, axis=axis, keepdims=True)
    spread = jnp.mean(jnp.square(values - center), axis=axis, keepdims=True)
    return (values - center) * lax.rsqrt(spread + 1e-05)


def dot(a, b, a_dim=1, b_dim=0):
    return lax.dot_general(a, b, (((a_dim,), (b_dim,)), ((), ())), preferred_element_type=F32)


def transposed(ref):
    return ref[...].astype(F32).T.astype(BF16)


def remote(src, dst, send_sem, recv_sem, row, chan):
    return pltpu.make_async_remote_copy(
        src_ref=src,
        dst_ref=dst,
        send_sem=send_sem,
        recv_sem=recv_sem,
        device_id=(row, chan),
        device_id_type=MESH,
    )


def block_kernel(
    pair_ref,
    mask_ref,
    alive_ref,
    left_proj_ref,
    left_gate_ref,
    right_proj_ref,
    right_gate_ref,
    mult_gate_ref,
    mult_out_ref,
    query_ref,
    key_ref,
    value_ref,
    bias_weight_ref,
    heads_gate_ref,
    heads_out_ref,
    swish_ref,
    linear_ref,
    project_ref,
    out_ref,
    left_f,
    right_f,
    normed0,
    send,
    mine,
    theirs,
    left_all,
    right_all,
    total,
    product,
    back,
    gate_f,
    norm_f,
    after_all,
    everything,
    bias_f,
    bias_send,
    bias_mine,
    bias_theirs,
    table,
    attended_f,
    edge_send,
    edge_recv,
    swap_send,
    swap_recv,
    back_send,
    back_recv,
    gather_send,
    gather_recv,
    bias_sem,
):
    rows, columns, channels = pair_ref.shape
    groups = rows // GROUP
    heads = bias_weight_ref.shape[0]
    row, chan = lax.axis_index("row"), lax.axis_index("chan")
    core, down = row % 2, row // 2
    zone, place = chan // 4, chan % 4
    here = down * 8 + chan
    pad = jnp.zeros((GROUP, 128 - columns, channels), BF16)

    def chip(step):
        dx, dz, dd = step // 32, (step // 16) % 2, step % 16
        return (down + dd) % 16, (zone + dz) % 2, (place + dx) % 4

    barrier = pltpu.get_barrier_semaphore()

    def greet(step):
        d, z, x = chip(step)
        pl.semaphore_signal(
            barrier, inc=1, device_id=(d * 2 + core, z * 4 + x), device_id_type=MESH
        )

    pl.semaphore_signal(
        barrier, inc=1, device_id=(row + 1 - 2 * core, chan), device_id_type=MESH
    )
    lax.fori_loop(1, 128, lambda step, carry: (greet(step), carry)[1], 0)

    weights = jnp.concatenate(
        [transposed(ref) for ref in (left_gate_ref, left_proj_ref, right_gate_ref, right_proj_ref)],
        axis=0,
    )

    def edges(g, carry):
        at = pl.ds(g * GROUP, GROUP)
        normed = normalize(pair_ref[at].astype(F32), 2).astype(BF16)
        normed0[at] = normed
        padded = jnp.concatenate([normed, pad], axis=1).reshape(GROUP * 128, channels)
        out = dot(weights, padded, 1, 1)
        for t in range(GROUP):
            lanes = slice(t * 128, (t + 1) * 128)
            mask = mask_ref[g * GROUP + t]
            to = pl.ds(pl.multiple_of((g * GROUP + t) * channels, channels), channels)
            left_f[to, :] = mask * jax.nn.sigmoid(out[0:128, lanes]) * out[128:256, lanes]
            right_f[to, :] = mask * jax.nn.sigmoid(out[256:384, lanes]) * out[384:512, lanes]
        return carry

    lax.fori_loop(0, groups, edges, 0)
    pl.semaphore_wait(barrier, 128)

    def edge_block(channel):
        at = pl.ds(channel, rows, stride=channels)
        return jnp.concatenate([right_f[at, :], left_f[at, :]], axis=0).astype(BF16)

    def edge_out(step, carry):
        d, z, x = chip(step)
        channel = d * 8 + z * 4 + x
        send[channel] = edge_block(channel)
        phase = step // 32
        remote(
            send.at[channel],
            mine.at[place, zone * 16 + down],
            edge_send.at[0],
            edge_recv.at[phase],
            d * 2 + core,
            z * 4 + x,
        ).start()
        return carry

    lax.fori_loop(1, 128, edge_out, 0)
    mine[place, zone * 16 + down] = edge_block(here)

    def gates(g, carry):
        at = pl.ds(g * GROUP, GROUP)
        normed = normed0[at].reshape(GROUP * columns, channels)
        gate = jax.nn.sigmoid(dot(normed, mult_gate_ref[...]))
        gate_f[at] = gate.reshape(GROUP, columns, channels)
        return carry

    lax.fori_loop(0, groups, gates, 0)

    def swap(phase):
        source = (place + 4 - phase) % 4
        return remote(
            mine.at[source, :, pl.ds(0, 32), :],
            theirs.at[source],
            swap_send.at[phase],
            swap_recv.at[phase],
            row + 1 - 2 * core,
            chan,
        )

    def arrive(phase):
        count = 31 if phase == 0 else 32
        arrived = mine.at[0, pl.ds(0, count)]
        pltpu.make_async_copy(arrived, arrived, edge_recv.at[phase]).wait()
        swap(phase).start()

    def stage(phase):
        source = (place + 4 - phase) % 4
        for z in range(2):
            lanes = slice(z * 128, (z + 1) * 128)
            mine_z = mine[source, z * 16 : (z + 1) * 16]
            left_all[:, lanes] = mine_z[:, 16:48].reshape(512, 128)
            own = mine_z[:, 0:32].reshape(4, 2, 64, 128)
            other = theirs[source, z * 16 : (z + 1) * 16].reshape(4, 2, 64, 128)
            for half in range(2):
                right_all[:, half * 128 : half * 128 + 64, lanes] = own[:, half]
                right_all[:, half * 128 + 64 : half * 128 + 128, lanes] = other[:, half]

    arrive(0)
    for phase in range(3):
        swap(phase).wait_recv()
        stage(phase)
        for pair in range(4):
            out = dot(left_all[...], right_all[pair], 1, 1)
            total[pair] = out if phase == 0 else total[pair] + out
        arrive(phase + 1)
    swap(3).wait_recv()
    stage(3)

    for turn in (1, 2, 3, 0):
        pair = (chan // 2 + turn) % 4
        out = total[pair] + dot(left_all[...], right_all[pair], 1, 1)
        for side in range(2):
            block = out[:, side * 128 : (side + 1) * 128].reshape(16, 32, 128)
            product[pair * 2 + side] = block[:, 8:32].astype(BF16)

        def back_out(step, carry):
            d, c = (down + step // 2) % 16, pair * 2 + (chan + step) % 2

            @pl.when(d * 8 + c != here)
            def _():
                remote(
                    product.at[c, d],
                    back.at[here],
                    back_send.at[0],
                    back_recv.at[0],
                    d * 2 + core,
                    c,
                ).start()

            return carry

        lax.fori_loop(0, 32, back_out, 0)
    back[here] = product[chan, down]
    bias_weights = jnp.concatenate(
        [bias_weight_ref[...].astype(F32), jnp.zeros((8 - heads, channels), F32)], axis=0
    ).astype(BF16)
    arrived = back.at[pl.ds(0, 127)]
    pltpu.make_async_copy(arrived, arrived, back_recv.at[0]).wait()

    def add(channel, carry):
        return carry + back[channel].astype(F32)

    zero = jnp.zeros((rows, 128), F32)
    center = lax.fori_loop(0, channels, add, zero, unroll=8) * (1.0 / channels)

    def square(channel, carry):
        return carry + jnp.square(back[channel].astype(F32) - center)

    spread = lax.fori_loop(0, channels, square, zero, unroll=8) * (1.0 / channels)
    scale = lax.rsqrt(spread + 1e-05)

    def scaled(channel, carry):
        at = pl.ds(pl.multiple_of(channel * rows, 8), rows)
        norm_f[at, :] = (back[channel].astype(F32) - center) * scale
        return carry

    lax.fori_loop(0, channels, scaled, 0, unroll=8)

    right, left = (place + 1) % 4, (place + 3) % 4

    def hop(slot, g):
        whole = pl.ds(g * GROUP, GROUP)
        first = pl.ds(g * GROUP, GROUP // 2)
        second = pl.ds(g * GROUP + GROUP // 2, GROUP // 2)
        other = 1 - zone
        source, part, z, x = (
            (chan, whole, other, place),
            (chan, whole, zone, right),
            (chan, whole, zone, left),
            (other * 4 + place, whole, zone, right),
            (other * 4 + place, whole, zone, left),
            (zone * 4 + left, first, zone, right),
            (zone * 4 + right, second, zone, left),
            (other * 4 + left, first, zone, right),
            (other * 4 + right, second, zone, left),
        )[slot]
        ref = everything.at[source, part]
        return remote(ref, ref, gather_send.at[slot, g], gather_recv.at[slot, g], row, z * 4 + x)

    def relay_across(g):
        hop(0, g).wait_recv()
        hop(3, g).start()
        hop(4, g).start()
        hop(1, g).wait_recv()
        hop(5, g).start()
        hop(2, g).wait_recv()
        hop(6, g).start()

    def relay_far(g):
        hop(3, g).wait_recv()
        hop(7, g).start()
        hop(4, g).wait_recv()
        hop(8, g).start()

    def finish(g, carry):
        at = pl.ds(g * GROUP, GROUP)
        lines = []
        for t in range(GROUP):
            product_norm = norm_f[pl.ds(g * GROUP + t, channels, stride=rows), :].astype(BF16)
            out = dot(product_norm, mult_out_ref[...], 0, 0)
            a, b, c, d = (out[32 * k : 32 * k + rows] for k in range(4))
            first = core == 0
            lines.append(
                jnp.concatenate(
                    [
                        jnp.where(first, a, c),
                        jnp.where(first, c, a),
                        jnp.where(first, b, d),
                        jnp.where(first, d, b),
                    ],
                    axis=0,
                )
            )
        update = jnp.concatenate(lines, axis=0).reshape(GROUP, columns, channels)
        after = (pair_ref[at].astype(F32) + gate_f[at] * update).astype(BF16)
        after_all[at] = after
        normed = normalize(after.astype(F32), 2).astype(BF16)
        everything[chan, at] = normed
        for slot in range(3):
            hop(slot, g).start()
        padded = jnp.concatenate([normed, pad], axis=1).reshape(GROUP * 128, channels)
        bias = dot(bias_weights, padded, 1, 1)
        for t in range(GROUP):
            to = pl.ds(pl.multiple_of((g * GROUP + t) * 8, 8), 8)
            bias_f[to, :] = bias[:, t * 128 : (t + 1) * 128]
        return carry

    lax.fori_loop(0, groups, finish, 0)

    lane = lax.broadcasted_iota(jnp.int32, (rows, 128), 1)
    spare = bias_f[pl.ds(heads - 1, rows, stride=8), :]
    for h in range(heads - 1):
        line = bias_f[pl.ds(h, rows, stride=8), :]
        bias_send[h] = jnp.where(lane < columns, line, pltpu.roll(spare, columns - 32 * h, 1))
    column, part = row // 4, (row % 4) // 2
    landing = bias_mine.at[part, chan]

    def bias_out(d):
        return remote(
            bias_send, landing, bias_sem.at[0], bias_sem.at[1], d * 2 + core, column
        )

    def bias_start(step, carry):
        d = (down + step) % 16
        stays = jnp.logical_and(d == down, chan == column)

        @pl.when(stays)
        def _():
            pltpu.make_async_copy(bias_send, landing, bias_sem.at[1]).start()

        @pl.when(jnp.logical_not(stays))
        def _():
            bias_out(d).start()

        return carry

    lax.fori_loop(0, 16, bias_start, 0)
    bias_swap = remote(
        bias_mine, bias_theirs, bias_sem.at[2], bias_sem.at[3], row + 1 - 2 * core, chan
    )
    for g in range(3):
        relay_across(g)
    pltpu.make_async_copy(bias_mine, bias_mine, bias_sem.at[1]).wait()
    bias_swap.start()
    relay_far(0)
    alive = alive_ref[...] > 0.5
    pieces = 128 - columns

    def assemble(ref, side):
        for p in range(2):
            for h in range(heads):
                if h < heads - 1:
                    parts = [ref[p, c, h][:, 0:columns] for c in range(8)]
                else:
                    parts = [
                        ref[p, c, k][:, columns:128] for c in range(8) for k in range(columns // pieces)
                    ]
                line = jnp.concatenate(parts, axis=1)
                table[h, 2 * p + side] = jnp.where(alive, line * LOG2E, -1e30)

    assemble(bias_mine, core)
    bias_swap.wait_recv()
    assemble(bias_theirs, 1 - core)
    relay_far(1)

    keys = table.shape[3]
    head_of_lane = lax.broadcasted_iota(jnp.int32, (columns, channels), 1) // (channels // heads)
    score_scale = LOG2E / math.sqrt(channels // heads)
    ones = jnp.ones((keys, channels), BF16)

    def attend(g, carry):
        for slot in (5, 6, 7, 8):
            hop(slot, g).wait_recv()

        @pl.when(g + 3 < groups)
        def _():
            relay_across(g + 3)

        @pl.when(g + 2 < groups)
        def _():
            relay_far(g + 2)

        at = pl.ds(g * GROUP, GROUP)
        key_value = jnp.concatenate([key_ref[...], value_ref[...]], axis=1)
        for t in range(GROUP):
            i = g * GROUP + t
            tokens = jnp.concatenate([everything[c, i] for c in range(8)], axis=0)
            projected = dot(tokens, key_value).astype(BF16)
            key, value = projected[:, 0:channels], projected[:, channels:]
            query = dot(everything[chan, i], query_ref[...])
            split = jnp.concatenate(
                [jnp.where(head_of_lane == h, query, 0.0) for h in range(heads)], axis=0
            ).astype(BF16)
            score = dot(split, key, 1, 1) * score_scale + table[...].reshape(heads * columns, keys)
            raised = jnp.exp2(score - jnp.max(score, axis=1, keepdims=True)).astype(BF16)
            summed = dot(raised, jnp.concatenate([value, ones], axis=1))
            top = jnp.zeros((columns, channels), F32)
            bottom = jnp.ones((columns, channels), F32)
            for h in range(heads):
                mine_h = slice(h * columns, (h + 1) * columns)
                top = jnp.where(head_of_lane == h, summed[mine_h, 0:channels], top)
                bottom = jnp.where(head_of_lane == h, summed[mine_h, channels:], bottom)
            attended_f[pl.ds(t * columns, columns), :] = top / bottom

        normed = everything[chan, at].reshape(GROUP * columns, channels)
        gate = jax.nn.sigmoid(dot(normed, heads_gate_ref[...]))
        mixed = (gate * attended_f[...]).astype(BF16)
        after = after_all[at].reshape(GROUP * columns, channels).astype(F32)
        second = (after + dot(mixed, heads_out_ref[...])).astype(BF16)
        second_f = second.astype(F32)
        normed = normalize(second_f, 1).astype(BF16)
        hidden = jax.nn.silu(dot(normed, swish_ref[...])) * dot(normed, linear_ref[...])
        out = (second_f + dot(hidden.astype(BF16), project_ref[...])).astype(BF16)
        out_ref[at] = out.reshape(GROUP, columns, channels)
        return carry

    lax.fori_loop(0, groups, attend, 0)

    sent = send.at[pl.ds(0, 127)]
    pltpu.make_async_copy(sent, sent, edge_send.at[0]).wait()
    sent = back.at[pl.ds(0, 127)]
    pltpu.make_async_copy(sent, sent, back_send.at[0]).wait()
    for phase in range(4):
        swap(phase).wait_send()
    bias_swap.wait_send()

    def bias_wait(step, carry):
        d = (down + step) % 16

        @pl.when(jnp.logical_not(jnp.logical_and(d == down, chan == column)))
        def _():
            bias_out(d).wait_send()

        return carry

    lax.fori_loop(0, 16, bias_wait, 0)

    def gather_wait(g, carry):
        for slot in range(9):
            hop(slot, g).wait_send()
        return carry

    lax.fori_loop(0, groups, gather_wait, 0)


def body(
    pair_input,
    token_valid,
    left_proj,
    left_gate,
    right_proj,
    right_gate,
    mult_gate,
    mult_out,
    query_weight,
    key_weight,
    value_weight,
    bias_weight,
    heads_gate,
    heads_out,
    swish_in,
    linear_in,
    project_out,
):
    rows, columns, channels = pair_input.shape
    heads = bias_weight.shape[1]
    tokens = token_valid.shape[0]
    row, chan = lax.axis_index("row"), lax.axis_index("chan")
    validity = token_valid.astype(F32)
    row_valid = lax.dynamic_slice_in_dim(validity, row * rows, rows)
    column_valid = lax.dynamic_slice_in_dim(validity, chan * columns, columns)
    column_valid = jnp.pad(column_valid, (0, 128 - columns))
    mask = (row_valid[:, None] * column_valid[None, :]).reshape(rows, 1, 128)
    groups = rows // GROUP
    return pl.pallas_call(
        block_kernel,
        out_shape=jax.ShapeDtypeStruct((rows, columns, channels), BF16),
        in_specs=[VMEM] * 18,
        out_specs=VMEM,
        scratch_shapes=[
            pltpu.VMEM((rows * channels, 128), F32),
            pltpu.VMEM((rows * channels, 128), F32),
            pltpu.VMEM((rows, columns, channels), BF16),
            pltpu.VMEM((128, 2 * rows, 128), BF16),
            pltpu.VMEM((4, 32, 2 * rows, 128), BF16),
            pltpu.VMEM((4, 32, 32, 128), BF16),
            pltpu.VMEM((512, 256), BF16),
            pltpu.VMEM((4, 256, 256), BF16),
            pltpu.VMEM((4, 512, 256), F32),
            pltpu.VMEM((8, 16, rows, 128), BF16),
            pltpu.VMEM((128, rows, 128), BF16),
            pltpu.VMEM((rows, columns, channels), F32),
            pltpu.VMEM((channels * rows, 128), F32),
            pltpu.VMEM((rows, columns, channels), BF16),
            pltpu.VMEM((8, rows, columns, channels), BF16),
            pltpu.VMEM((rows * 8, 128), F32),
            pltpu.VMEM((heads - 1, rows, 128), F32),
            pltpu.VMEM((2, 8, heads - 1, rows, 128), F32),
            pltpu.VMEM((2, 8, heads - 1, rows, 128), F32),
            pltpu.VMEM((heads, 4, rows, tokens), F32),
            pltpu.VMEM((GROUP * columns, channels), F32),
            pltpu.SemaphoreType.DMA((1,)),
            pltpu.SemaphoreType.DMA((4,)),
            pltpu.SemaphoreType.DMA((4,)),
            pltpu.SemaphoreType.DMA((4,)),
            pltpu.SemaphoreType.DMA((1,)),
            pltpu.SemaphoreType.DMA((1,)),
            pltpu.SemaphoreType.DMA((9, groups)),
            pltpu.SemaphoreType.DMA((9, groups)),
            pltpu.SemaphoreType.DMA((4,)),
        ],
        compiler_params=pltpu.CompilerParams(
            collective_id=0, has_side_effects=True, vmem_limit_bytes=LIMIT
        ),
        name="block",
    )(
        pair_input,
        mask,
        validity.reshape(1, tokens),
        left_proj,
        left_gate,
        right_proj,
        right_gate,
        mult_gate,
        mult_out,
        query_weight,
        key_weight,
        value_weight,
        bias_weight.T,
        heads_gate,
        heads_out,
        swish_in,
        linear_in,
        project_out,
    )


def solution(mesh):
    return jax.shard_map(
        body,
        mesh=mesh,
        in_specs=(P("row", "chan", None),) + (P(),) * 16,
        out_specs=P("row", "chan", None),
        check_vma=False,
    )
```

```python
import math

import jax
import jax.numpy as jnp
from jax import lax
from jax.experimental import pallas as pl
from jax.experimental.pallas import tpu as pltpu
from jax.sharding import PartitionSpec as P

BF16 = jnp.bfloat16
F32 = jnp.float32
LOG2E = math.log2(math.e)
MESH = pl.DeviceIdType.MESH
VMEM = pl.BlockSpec(memory_space=pltpu.VMEM)
LIMIT = 60 * 1024 * 1024
GROUP = 4


def normalize(values, axis):
    center = jnp.mean(values, axis=axis, keepdims=True)
    spread = jnp.mean(jnp.square(values - center), axis=axis, keepdims=True)
    return (values - center) * lax.rsqrt(spread + 1e-05)


def dot(a, b, a_dim=1, b_dim=0):
    return lax.dot_general(a, b, (((a_dim,), (b_dim,)), ((), ())), preferred_element_type=F32)


def transposed(ref):
    return ref[...].astype(F32).T.astype(BF16)


def remote(src, dst, send_sem, recv_sem, row, chan):
    return pltpu.make_async_remote_copy(
        src_ref=src,
        dst_ref=dst,
        send_sem=send_sem,
        recv_sem=recv_sem,
        device_id=(row, chan),
        device_id_type=MESH,
    )


def block_kernel(
    pair_ref,
    token_ref,
    valid_ref,
    left_proj_ref,
    left_gate_ref,
    right_proj_ref,
    right_gate_ref,
    mult_gate_ref,
    mult_out_ref,
    query_ref,
    key_ref,
    value_ref,
    bias_weight_ref,
    heads_gate_ref,
    heads_out_ref,
    swish_ref,
    linear_ref,
    project_ref,
    out_ref,
    left_f,
    right_f,
    normed0,
    send,
    mine,
    theirs,
    left_first,
    left_rest,
    right_all,
    product_first,
    product_rest,
    back_first,
    back_rest,
    gate_f,
    norm_f,
    after_all,
    everything,
    bias_f,
    send_first,
    send_rest,
    mine_first,
    mine_rest,
    theirs_first,
    theirs_rest,
    table,
    attended_f,
    met_sem,
    edge_send,
    edge_recv,
    swap_send,
    swap_recv,
    back_send,
    back_recv,
    gather_send,
    gather_recv,
    bias_sem,
):
    rows, columns, channels = pair_ref.shape
    groups = rows // GROUP
    heads = bias_weight_ref.shape[0]
    row, chan = lax.axis_index("row"), lax.axis_index("chan")
    core, down = row % 2, row // 2
    zone, place = chan // 4, chan % 4
    here = down * 8 + chan
    pad = jnp.zeros((GROUP, 128 - columns, channels), BF16)

    def chip(step):
        dx, dz, dd = step // 32, (step // 16) % 2, step % 16
        return (down + dd) % 16, (zone + dz) % 2, (place + dx) % 4

    barrier = pltpu.get_barrier_semaphore()

    def signal(sem, d, c, r):
        pl.semaphore_signal(sem, inc=1, device_id=(d * 2 + r, c), device_id_type=MESH)

    signal(barrier, down, chan, 1 - core)
    for step in range(1, 16):
        signal(barrier, (down + step) % 16, chan, core)
    for step in range(1, 8):
        signal(barrier, down, (chan + step) % 8, core)

    weights = jnp.concatenate(
        [transposed(ref) for ref in (left_gate_ref, left_proj_ref, right_gate_ref, right_proj_ref)],
        axis=0,
    )

    column_mask = valid_ref[pl.ds(chan, 1), :]

    def edges(g, carry):
        at = pl.ds(g * GROUP, GROUP)
        normed = normalize(pair_ref[at].astype(F32), 2).astype(BF16)
        normed0[at] = normed
        padded = jnp.concatenate([normed, pad], axis=1).reshape(GROUP * 128, channels)
        out = dot(weights, padded, 1, 1)
        for t in range(GROUP):
            lanes = slice(t * 128, (t + 1) * 128)
            mask = column_mask * token_ref[row * rows + g * GROUP + t].astype(F32)
            to = pl.ds(pl.multiple_of((g * GROUP + t) * channels, channels), channels)
            left_f[to, :] = mask * jax.nn.sigmoid(out[0:128, lanes]) * out[128:256, lanes]
            right_f[to, :] = mask * jax.nn.sigmoid(out[256:384, lanes]) * out[384:512, lanes]
        return carry

    lax.fori_loop(0, groups // 2, edges, 0)
    pl.semaphore_wait(barrier, 23)
    for step in range(1, 8):
        signal(met_sem, down, (chan + step) % 8, core)
    lax.fori_loop(groups // 2, groups, edges, 0)
    pl.semaphore_wait(met_sem, 7)

    def edge_block(channel):
        at = pl.ds(channel, rows, stride=channels)
        return jnp.concatenate([right_f[at, :], left_f[at, :]], axis=0).astype(BF16)

    def edge_copy(step, part):
        d, z, x = chip(step)
        channel = d * 8 + z * 4 + x
        at = pl.ds(0, 32) if part == 0 else pl.ds(32, 16)
        phase = step // 32 if part == 0 else 4
        return remote(
            send.at[channel, at],
            mine.at[place, zone * 16 + down, at],
            edge_send.at[0],
            edge_recv.at[phase],
            d * 2 + core,
            z * 4 + x,
        )

    def edge_out(step, carry):
        d, z, x = chip(step)
        channel = d * 8 + z * 4 + x
        send[channel] = edge_block(channel)
        edge_copy(step, 0).start()
        return carry

    lax.fori_loop(1, 128, edge_out, 0)
    mine[place, zone * 16 + down] = edge_block(here)
    lax.fori_loop(1, 128, lambda step, carry: (edge_copy(step, 1).start(), carry)[1], 0)

    def gates(g, carry):
        at = pl.ds(g * GROUP, GROUP)
        normed = normed0[at].reshape(GROUP * columns, channels)
        gate = jax.nn.sigmoid(dot(normed, mult_gate_ref[...]))
        gate_f[at] = gate.reshape(GROUP, columns, channels)
        return carry

    lax.fori_loop(0, groups, gates, 0)

    def swap(phase):
        source = (place + 4 - phase) % 4
        return remote(
            mine.at[source, :, pl.ds(0, 32), :],
            theirs.at[source],
            swap_send.at[phase],
            swap_recv.at[phase],
            row + 1 - 2 * core,
            chan,
        )

    def arrive(phase):
        count = 31 if phase == 0 else 32
        arrived = mine.at[0, pl.ds(0, count), pl.ds(0, 32)]
        pltpu.make_async_copy(arrived, arrived, edge_recv.at[phase]).wait()
        swap(phase).start()

    def stage(phase):
        source = (place + 4 - phase) % 4
        for z in range(2):
            lanes = slice(phase * 256 + z * 128, phase * 256 + (z + 1) * 128)
            mine_z = mine[source, z * 16 : (z + 1) * 16, 0:32, :]
            left_first[:, lanes] = mine_z.astype(F32)[:, 24:32].reshape(128, 128).astype(BF16)
            own = mine_z.reshape(4, 2, 64, 128)
            other = theirs[source, z * 16 : (z + 1) * 16].reshape(4, 2, 64, 128)
            for half in range(2):
                right_all[:, half * 128 : half * 128 + 64, lanes] = own[:, half]
                right_all[:, half * 128 + 64 : half * 128 + 128, lanes] = other[:, half]

    for phase in range(4):
        arrive(phase)
        if phase > 0:
            swap(phase - 1).wait_recv()
            stage(phase - 1)
    swap(3).wait_recv()
    stage(3)

    def multiply(left, product, back, part, turn):
        pair = (chan // 2 + turn) % 4
        count = product.shape[2]
        out = dot(left[...], right_all[pair], 1, 1)
        for side in range(2):
            block = out[:, side * 128 : (side + 1) * 128].reshape(16, count, 128)
            product[pair * 2 + side] = block.astype(BF16)

        def back_out(step, carry):
            d, c = (down + step // 2) % 16, pair * 2 + (chan + step) % 2

            @pl.when(d * 8 + c != here)
            def _():
                remote(
                    product.at[c, d],
                    back.at[here],
                    back_send.at[part],
                    back_recv.at[part],
                    d * 2 + core,
                    c,
                ).start()

            return carry

        lax.fori_loop(0, 32, back_out, 0)

    for turn in (1, 2, 3, 0):
        multiply(left_first, product_first, back_first, 0, turn)
    back_first[here] = product_first[chan, down]
    arrived = back_rest.at[pl.ds(0, 127)]
    pltpu.make_async_copy(arrived, arrived, edge_recv.at[4]).wait()
    for phase in range(4):
        source = (place + 4 - phase) % 4
        for z in range(2):
            lanes = slice(phase * 256 + z * 128, phase * 256 + (z + 1) * 128)
            left_rest[:, lanes] = mine[source, z * 16 : (z + 1) * 16, 32:48, :].reshape(256, 128)
    for turn in (1, 2, 3, 0):
        multiply(left_rest, product_rest, back_rest, 1, turn)
    back_rest[here] = product_rest[chan, down]
    bias_weights = jnp.concatenate(
        [bias_weight_ref[...].astype(F32), jnp.zeros((8 - heads, channels), F32)], axis=0
    ).astype(BF16)

    def product_norms(back, part):
        count = back.shape[1]
        arrived = back.at[pl.ds(0, 127)]
        pltpu.make_async_copy(arrived, arrived, back_recv.at[part]).wait()

        def add(channel, carry):
            return carry + back[channel].astype(F32)

        zero = jnp.zeros((count, 128), F32)
        center = lax.fori_loop(0, channels, add, zero, unroll=8) * (1.0 / channels)

        def square(channel, carry):
            return carry + jnp.square(back[channel].astype(F32) - center)

        spread = lax.fori_loop(0, channels, square, zero, unroll=8) * (1.0 / channels)
        scale = lax.rsqrt(spread + 1e-05)

        def scaled(channel, carry):
            at = pl.ds(pl.multiple_of(channel * count, 8), count)
            norm_f[at, :] = (back[channel].astype(F32) - center) * scale
            return carry

        lax.fori_loop(0, channels, scaled, 0, unroll=8)

    right, left = (place + 1) % 4, (place + 3) % 4

    def hop(slot, g):
        whole = pl.ds(g * GROUP, GROUP)
        first = pl.ds(g * GROUP, GROUP // 2)
        second = pl.ds(g * GROUP + GROUP // 2, GROUP // 2)
        other = 1 - zone
        source, part, z, x = (
            (chan, whole, other, place),
            (chan, whole, zone, right),
            (chan, whole, zone, left),
            (other * 4 + place, whole, zone, right),
            (other * 4 + place, whole, zone, left),
            (zone * 4 + left, first, zone, right),
            (zone * 4 + right, second, zone, left),
            (other * 4 + left, first, zone, right),
            (other * 4 + right, second, zone, left),
        )[slot]
        ref = everything.at[source, part]
        return remote(ref, ref, gather_send.at[slot, g], gather_recv.at[slot, g], row, z * 4 + x)

    def relay_across(g):
        hop(0, g).wait_recv()
        hop(3, g).start()
        hop(4, g).start()
        hop(1, g).wait_recv()
        hop(5, g).start()
        hop(2, g).wait_recv()
        hop(6, g).start()

    def relay_far(g):
        hop(3, g).wait_recv()
        hop(7, g).start()
        hop(4, g).wait_recv()
        hop(8, g).start()

    def finish(g, first_row, count):
        at = pl.ds(g * GROUP, GROUP)
        lines = []
        for t in range(GROUP):
            line = norm_f[pl.ds(g * GROUP + t - first_row, channels, stride=count), :]
            product_norm = line.astype(BF16)
            out = dot(product_norm, mult_out_ref[...], 0, 0)
            a, b, c, d = (out[32 * k : 32 * k + rows] for k in range(4))
            first = core == 0
            lines.append(
                jnp.concatenate(
                    [
                        jnp.where(first, a, c),
                        jnp.where(first, c, a),
                        jnp.where(first, b, d),
                        jnp.where(first, d, b),
                    ],
                    axis=0,
                )
            )
        update = jnp.concatenate(lines, axis=0).reshape(GROUP, columns, channels)
        after = (pair_ref[at].astype(F32) + gate_f[at] * update).astype(BF16)
        after_all[at] = after
        normed = normalize(after.astype(F32), 2).astype(BF16)
        everything[chan, at] = normed
        for slot in range(3):
            hop(slot, g).start()
        padded = jnp.concatenate([normed, pad], axis=1).reshape(GROUP * 128, channels)
        bias = dot(bias_weights, padded, 1, 1)
        for t in range(GROUP):
            to = pl.ds(pl.multiple_of((g * GROUP + t) * 8, 8), 8)
            bias_f[to, :] = bias[:, t * 128 : (t + 1) * 128]

    column, half_of_four = row // 4, (row % 4) // 2
    pieces = 128 - columns

    def bias_copy(refs, part, d):
        return remote(
            refs[0],
            refs[1].at[half_of_four, chan],
            bias_sem.at[part, 0],
            bias_sem.at[part, 1],
            d * 2 + core,
            column,
        )

    def stays(d):
        return jnp.logical_and(d == down, chan == column)

    def bias_out(refs, part, first_row):
        count = refs[0].shape[1]
        lane = lax.broadcasted_iota(jnp.int32, (count, 128), 1)
        spare = bias_f[pl.ds(first_row * 8 + heads - 1, count, stride=8), :]
        for h in range(heads - 1):
            line = bias_f[pl.ds(first_row * 8 + h, count, stride=8), :]
            refs[0][h] = jnp.where(lane < columns, line, pltpu.roll(spare, columns - pieces * h, 1))

        def start(step, carry):
            d = (down + step) % 16

            @pl.when(stays(d))
            def _():
                pltpu.make_async_copy(
                    refs[0], refs[1].at[half_of_four, chan], bias_sem.at[part, 1]
                ).start()

            @pl.when(jnp.logical_not(stays(d)))
            def _():
                bias_copy(refs, part, d).start()

            return carry

        lax.fori_loop(0, 16, start, 0)

    def bias_drain(refs, part):
        def wait(step, carry):
            d = (down + step) % 16

            @pl.when(jnp.logical_not(stays(d)))
            def _():
                bias_copy(refs, part, d).wait_send()

            return carry

        lax.fori_loop(0, 16, wait, 0)

    def bias_swap(refs, part):
        return remote(
            refs[1], refs[2], bias_sem.at[part, 2], bias_sem.at[part, 3], row + 1 - 2 * core, chan
        )

    def bias_arrive(refs, part):
        pltpu.make_async_copy(refs[1], refs[1], bias_sem.at[part, 1]).wait()
        bias_swap(refs, part).start()

    alive = jnp.concatenate([valid_ref[c : c + 1, 0:columns] for c in range(8)], axis=1) > 0.5

    def assemble(ref, side, first_row):
        count = ref.shape[3]
        for p in range(2):
            for h in range(heads):
                if h < heads - 1:
                    parts = [ref[p, c, h][:, 0:columns] for c in range(8)]
                else:
                    parts = [
                        ref[p, c, k][:, columns:128]
                        for c in range(8)
                        for k in range(columns // pieces)
                    ]
                line = jnp.concatenate(parts, axis=1)
                table[h, 2 * p + side, first_row : first_row + count] = jnp.where(
                    alive, line * LOG2E, -1e30
                )

    early = (send_first, mine_first, theirs_first)
    late = (send_rest, mine_rest, theirs_rest)
    early_rows, late_rows = send_first.shape[1], send_rest.shape[1]
    early_groups = early_rows // GROUP

    product_norms(back_first, 0)
    for g in range(early_groups):
        finish(g, 0, early_rows)
    bias_out(early, 0, 0)
    relay_across(0)
    relay_across(1)
    product_norms(back_rest, 1)
    lax.fori_loop(
        early_groups, groups, lambda g, carry: (finish(g, early_rows, late_rows), carry)[1], 0
    )
    bias_out(late, 1, early_rows)
    bias_arrive(early, 0)
    relay_far(0)
    relay_far(1)
    relay_across(2)
    assemble(mine_first, core, 0)
    bias_swap(early, 0).wait_recv()
    assemble(theirs_first, 1 - core, 0)
    relay_across(3)
    bias_arrive(late, 1)
    relay_far(2)
    assemble(mine_rest, core, early_rows)
    bias_swap(late, 1).wait_recv()
    assemble(theirs_rest, 1 - core, early_rows)

    keys = table.shape[3]
    head_of_lane = lax.broadcasted_iota(jnp.int32, (columns, channels), 1) // (channels // heads)
    score_scale = LOG2E / math.sqrt(channels // heads)
    ones = jnp.ones((keys, channels), BF16)

    def attend(g, carry):
        for slot in (5, 6, 7, 8):
            hop(slot, g).wait_recv()

        @pl.when(g + 4 < groups)
        def _():
            relay_across(g + 4)

        @pl.when(g + 3 < groups)
        def _():
            relay_far(g + 3)

        at = pl.ds(g * GROUP, GROUP)
        key_value = jnp.concatenate([key_ref[...], value_ref[...]], axis=1)
        for t in range(GROUP):
            i = g * GROUP + t
            tokens = jnp.concatenate([everything[c, i] for c in range(8)], axis=0)
            projected = dot(tokens, key_value).astype(BF16)
            key, value = projected[:, 0:channels], projected[:, channels:]
            query = dot(everything[chan, i], query_ref[...])
            split = jnp.concatenate(
                [jnp.where(head_of_lane == h, query, 0.0) for h in range(heads)], axis=0
            ).astype(BF16)
            score = dot(split, key, 1, 1) * score_scale + table[...].reshape(heads * columns, keys)
            raised = jnp.exp2(score - jnp.max(score, axis=1, keepdims=True)).astype(BF16)
            summed = dot(raised, jnp.concatenate([value, ones], axis=1))
            top = jnp.zeros((columns, channels), F32)
            bottom = jnp.ones((columns, channels), F32)
            for h in range(heads):
                mine_h = slice(h * columns, (h + 1) * columns)
                top = jnp.where(head_of_lane == h, summed[mine_h, 0:channels], top)
                bottom = jnp.where(head_of_lane == h, summed[mine_h, channels:], bottom)
            attended_f[pl.ds(t * columns, columns), :] = top / bottom

        normed = everything[chan, at].reshape(GROUP * columns, channels)
        gate = jax.nn.sigmoid(dot(normed, heads_gate_ref[...]))
        mixed = (gate * attended_f[...]).astype(BF16)
        after = after_all[at].reshape(GROUP * columns, channels).astype(F32)
        second = (after + dot(mixed, heads_out_ref[...])).astype(BF16)
        second_f = second.astype(F32)
        normed = normalize(second_f, 1).astype(BF16)
        hidden = jax.nn.silu(dot(normed, swish_ref[...])) * dot(normed, linear_ref[...])
        out = (second_f + dot(hidden.astype(BF16), project_ref[...])).astype(BF16)
        out_ref[at] = out.reshape(GROUP, columns, channels)
        return carry

    lax.fori_loop(0, groups, attend, 0)

    sent = send.at[pl.ds(0, 127)]
    pltpu.make_async_copy(sent, sent, edge_send.at[0]).wait()
    for part, (back, refs) in enumerate(((back_first, early), (back_rest, late))):
        sent = back.at[pl.ds(0, 127)]
        pltpu.make_async_copy(sent, sent, back_send.at[part]).wait()
        bias_swap(refs, part).wait_send()
        bias_drain(refs, part)
    for phase in range(4):
        swap(phase).wait_send()

    def gather_wait(g, carry):
        for slot in range(9):
            hop(slot, g).wait_send()
        return carry

    lax.fori_loop(0, groups, gather_wait, 0)


def body(
    pair_input,
    token_valid,
    left_proj,
    left_gate,
    right_proj,
    right_gate,
    mult_gate,
    mult_out,
    query_weight,
    key_weight,
    value_weight,
    bias_weight,
    heads_gate,
    heads_out,
    swish_in,
    linear_in,
    project_out,
):
    rows, columns, channels = pair_input.shape
    heads = bias_weight.shape[1]
    tokens = token_valid.shape[0]
    valid = jnp.pad(
        token_valid.astype(F32).reshape(tokens // columns, columns), ((0, 0), (0, 128 - columns))
    )
    groups = rows // GROUP
    return pl.pallas_call(
        block_kernel,
        out_shape=jax.ShapeDtypeStruct((rows, columns, channels), BF16),
        in_specs=[VMEM, pl.BlockSpec(memory_space=pltpu.SMEM)] + [VMEM] * 16,
        out_specs=VMEM,
        scratch_shapes=[
            pltpu.VMEM((rows * channels, 128), F32),
            pltpu.VMEM((rows * channels, 128), F32),
            pltpu.VMEM((rows, columns, channels), BF16),
            pltpu.VMEM((128, 2 * rows, 128), BF16),
            pltpu.VMEM((4, 32, 2 * rows, 128), BF16),
            pltpu.VMEM((4, 32, 32, 128), BF16),
            pltpu.VMEM((128, 1024), BF16),
            pltpu.VMEM((256, 1024), BF16),
            pltpu.VMEM((4, 256, 1024), BF16),
            pltpu.VMEM((8, 16, 8, 128), BF16),
            pltpu.VMEM((8, 16, 16, 128), BF16),
            pltpu.VMEM((128, 8, 128), BF16),
            pltpu.VMEM((128, 16, 128), BF16),
            pltpu.VMEM((rows, columns, channels), F32),
            pltpu.VMEM((channels * 16, 128), F32),
            pltpu.VMEM((rows, columns, channels), BF16),
            pltpu.VMEM((8, rows, columns, channels), BF16),
            pltpu.VMEM((rows * 8, 128), F32),
            pltpu.VMEM((heads - 1, 8, 128), F32),
            pltpu.VMEM((heads - 1, 16, 128), F32),
            pltpu.VMEM((2, 8, heads - 1, 8, 128), F32),
            pltpu.VMEM((2, 8, heads - 1, 16, 128), F32),
            pltpu.VMEM((2, 8, heads - 1, 8, 128), F32),
            pltpu.VMEM((2, 8, heads - 1, 16, 128), F32),
            pltpu.VMEM((heads, 4, rows, tokens), F32),
            pltpu.VMEM((GROUP * columns, channels), F32),
            pltpu.SemaphoreType.REGULAR,
            pltpu.SemaphoreType.DMA((1,)),
            pltpu.SemaphoreType.DMA((5,)),
            pltpu.SemaphoreType.DMA((4,)),
            pltpu.SemaphoreType.DMA((4,)),
            pltpu.SemaphoreType.DMA((2,)),
            pltpu.SemaphoreType.DMA((2,)),
            pltpu.SemaphoreType.DMA((9, groups)),
            pltpu.SemaphoreType.DMA((9, groups)),
            pltpu.SemaphoreType.DMA((2, 4)),
        ],
        compiler_params=pltpu.CompilerParams(
            collective_id=0, has_side_effects=True, vmem_limit_bytes=LIMIT
        ),
        name="block",
    )(
        pair_input,
        token_valid,
        valid,
        left_proj,
        left_gate,
        right_proj,
        right_gate,
        mult_gate,
        mult_out,
        query_weight,
        key_weight,
        value_weight,
        bias_weight.T,
        heads_gate,
        heads_out,
        swish_in,
        linear_in,
        project_out,
    )


def solution(mesh):
    return jax.shard_map(
        body,
        mesh=mesh,
        in_specs=(P("row", "chan", None),) + (P(),) * 16,
        out_specs=P("row", "chan", None),
        check_vma=False,
    )
```

```python
import math

import jax
import jax.numpy as jnp
from jax import lax
from jax.experimental import pallas as pl
from jax.experimental.pallas import tpu as pltpu
from jax.sharding import PartitionSpec as P

BF16 = jnp.bfloat16
F32 = jnp.float32
LOG2E = math.log2(math.e)
MESH = pl.DeviceIdType.MESH
VMEM = pl.BlockSpec(memory_space=pltpu.VMEM)
LIMIT = 60 * 1024 * 1024
GROUP = 4


def normalize(values, axis):
    center = jnp.mean(values, axis=axis, keepdims=True)
    spread = jnp.mean(jnp.square(values - center), axis=axis, keepdims=True)
    return (values - center) * lax.rsqrt(spread + 1e-05)


def dot(a, b, a_dim=1, b_dim=0):
    return lax.dot_general(a, b, (((a_dim,), (b_dim,)), ((), ())), preferred_element_type=F32)


def transposed(ref):
    return ref[...].astype(F32).T.astype(BF16)


def remote(src, dst, send_sem, recv_sem, row, chan):
    return pltpu.make_async_remote_copy(
        src_ref=src,
        dst_ref=dst,
        send_sem=send_sem,
        recv_sem=recv_sem,
        device_id=(row, chan),
        device_id_type=MESH,
    )


def block_kernel(
    pair_ref,
    token_ref,
    valid_ref,
    left_proj_ref,
    left_gate_ref,
    right_proj_ref,
    right_gate_ref,
    mult_gate_ref,
    mult_out_ref,
    query_ref,
    key_ref,
    value_ref,
    bias_weight_ref,
    heads_gate_ref,
    heads_out_ref,
    swish_ref,
    linear_ref,
    project_ref,
    out_ref,
    left_f,
    right_f,
    normed0,
    send_first,
    send_rest,
    mine_first,
    mine_rest,
    theirs,
    left_first,
    left_rest,
    right_all,
    product,
    back,
    gate_f,
    norm_f,
    after_all,
    everything,
    bias_f,
    bias_send,
    bias_mine,
    bias_theirs,
    table,
    attended_f,
    met_sem,
    edge_send,
    edge_recv,
    swap_send,
    swap_recv,
    back_send,
    back_recv,
    gather_send,
    gather_recv,
    bias_out_sem,
    bias_in_sem,
    bias_swap_out,
    bias_swap_in,
):
    rows, columns, channels = pair_ref.shape
    groups = rows // GROUP
    heads = bias_weight_ref.shape[0]
    row, chan = lax.axis_index("row"), lax.axis_index("chan")
    core, down = row % 2, row // 2
    zone, place = chan // 4, chan % 4
    here = down * 8 + chan
    pad = jnp.zeros((GROUP, 128 - columns, channels), BF16)

    def chip(step):
        dx, dz, dd = step // 32, (step // 16) % 2, step % 16
        return (down + dd) % 16, (zone + dz) % 2, (place + dx) % 4

    barrier = pltpu.get_barrier_semaphore()

    def signal(sem, d, c, r):
        pl.semaphore_signal(sem, inc=1, device_id=(d * 2 + r, c), device_id_type=MESH)

    signal(barrier, down, chan, 1 - core)
    for step in range(1, 16):
        signal(barrier, (down + step) % 16, chan, core)
    for step in range(1, 8):
        signal(barrier, down, (chan + step) % 8, core)

    weights = jnp.concatenate(
        [transposed(ref) for ref in (left_gate_ref, left_proj_ref, right_gate_ref, right_proj_ref)],
        axis=0,
    )

    column_mask = valid_ref[pl.ds(chan, 1), :]

    def edges(g, carry):
        at = pl.ds(g * GROUP, GROUP)
        normed = normalize(pair_ref[at].astype(F32), 2).astype(BF16)
        normed0[at] = normed
        padded = jnp.concatenate([normed, pad], axis=1).reshape(GROUP * 128, channels)
        out = dot(weights, padded, 1, 1)
        for t in range(GROUP):
            lanes = slice(t * 128, (t + 1) * 128)
            mask = column_mask * token_ref[row * rows + g * GROUP + t].astype(F32)
            to = pl.ds(pl.multiple_of((g * GROUP + t) * channels, channels), channels)
            left_f[to, :] = mask * jax.nn.sigmoid(out[0:128, lanes]) * out[128:256, lanes]
            right_f[to, :] = mask * jax.nn.sigmoid(out[256:384, lanes]) * out[384:512, lanes]
        return carry

    lax.fori_loop(0, groups // 2, edges, 0)
    pl.semaphore_wait(barrier, 23)
    for step in range(1, 8):
        signal(met_sem, down, (chan + step) % 8, core)
    lax.fori_loop(groups // 2, groups, edges, 0)
    pl.semaphore_wait(met_sem, 7)

    lane = lax.broadcasted_iota(jnp.int32, (8, 128), 1)
    piece = 128 - columns

    def edge_blocks(channel):
        at = pl.ds(channel, rows, stride=channels)
        right, left = right_f[at, :], left_f[at, :]
        packed = [
            jnp.where(
                lane < columns,
                right[8 * k : 8 * k + 8],
                pltpu.roll(left[0:8], columns - piece * k, 1),
            )
            for k in range(3)
        ]
        return jnp.concatenate(packed, axis=0).astype(BF16), left[8:rows].astype(BF16)

    def edge_copy(step, part):
        d, z, x = chip(step)
        channel = d * 8 + z * 4 + x
        send, mine = ((send_first, mine_first), (send_rest, mine_rest))[part]
        return remote(
            send.at[channel],
            mine.at[place, zone * 16 + down],
            edge_send.at[part],
            edge_recv.at[step // 32 if part == 0 else 4],
            d * 2 + core,
            z * 4 + x,
        )

    def edge_out(step, carry):
        d, z, x = chip(step)
        channel = d * 8 + z * 4 + x
        send_first[channel], send_rest[channel] = edge_blocks(channel)
        edge_copy(step, 0).start()
        return carry

    lax.fori_loop(1, 128, edge_out, 0)
    mine_first[place, zone * 16 + down], mine_rest[place, zone * 16 + down] = edge_blocks(here)
    lax.fori_loop(1, 128, lambda step, carry: (edge_copy(step, 1).start(), carry)[1], 0)

    def gates(g, carry):
        at = pl.ds(g * GROUP, GROUP)
        normed = normed0[at].reshape(GROUP * columns, channels)
        gate = jax.nn.sigmoid(dot(normed, mult_gate_ref[...]))
        gate_f[at] = gate.reshape(GROUP, columns, channels)
        return carry

    lax.fori_loop(0, groups, gates, 0)

    def swap(phase):
        source = (place + 4 - phase) % 4
        return remote(
            mine_first.at[source],
            theirs.at[source],
            swap_send.at[phase],
            swap_recv.at[phase],
            row + 1 - 2 * core,
            chan,
        )

    def arrive(phase):
        arrived = mine_first.at[0, pl.ds(0, 31 if phase == 0 else 32)]
        pltpu.make_async_copy(arrived, arrived, edge_recv.at[phase]).wait()
        swap(phase).start()

    right_all[:, columns:128] = jnp.zeros((8, piece, 1024), BF16)
    lanes_of = lax.broadcasted_iota(jnp.int32, (128, 128), 1)

    def stage(phase):
        source = (place + 4 - phase) % 4
        for z in range(2):
            lanes = slice(phase * 256 + z * 128, phase * 256 + (z + 1) * 128)
            own = mine_first[source, z * 16 : (z + 1) * 16].astype(F32)
            other = theirs[source, z * 16 : (z + 1) * 16].astype(F32)
            both = jnp.concatenate([own.reshape(8, 48, 128), other.reshape(8, 48, 128)], axis=1)
            right_all[:, 0:columns, lanes] = both.astype(BF16)
            left = jnp.zeros((128, 128), F32)
            for k in range(3):
                turned = pltpu.roll(
                    own[:, 8 * k : 8 * k + 8].reshape(128, 128), piece + piece * k, 1
                )
                left = jnp.where(lanes_of // piece == k, turned, left)
            left_first[:, lanes] = left.astype(BF16)

    for phase in range(4):
        arrive(phase)
        if phase > 0:
            swap(phase - 1).wait_recv()
            stage(phase - 1)
    swap(3).wait_recv()
    stage(3)

    def back_out(part, turn):
        pair = (chan // 2 + turn) % 4

        def start(step, carry):
            d, c = (down + step // 2) % 16, pair * 2 + (chan + step) % 2

            @pl.when(d * 8 + c != here)
            def _():
                remote(
                    product.at[part, c, d],
                    back.at[part, here],
                    back_send.at[part],
                    back_recv.at[part],
                    d * 2 + core,
                    c,
                ).start()

            return carry

        lax.fori_loop(0, 32, start, 0)

    def multiply(left, first_part, turn):
        pair = (chan // 2 + turn) % 4
        right = right_all[pl.ds(pair * 2, 2)].reshape(256, 1024)
        out = dot(left[...], right, 1, 1)
        for side in range(2):
            block = out[:, side * 128 : (side + 1) * 128].reshape(16, -1, 128)
            for k in range(block.shape[1] // 8):
                product[first_part + k, pair * 2 + side] = block[:, 8 * k : 8 * k + 8].astype(BF16)
        back_out(first_part, turn)

    turns = (1, 2, 3, 0)
    for turn in turns:
        multiply(left_first, 0, turn)
    arrived = send_rest.at[pl.ds(0, 127)]
    pltpu.make_async_copy(arrived, arrived, edge_recv.at[4]).wait()
    for phase in range(4):
        source = (place + 4 - phase) % 4
        for z in range(2):
            lanes = slice(phase * 256 + z * 128, phase * 256 + (z + 1) * 128)
            left_rest[:, lanes] = mine_rest[source, z * 16 : (z + 1) * 16].reshape(256, 128)
    for turn in turns:
        multiply(left_rest, 1, turn)
    for turn in turns:
        back_out(2, turn)
    for part in range(3):
        back[part, here] = product[part, chan, down]
    bias_weights = jnp.concatenate(
        [bias_weight_ref[...].astype(F32), jnp.zeros((8 - heads, channels), F32)], axis=0
    ).astype(BF16)

    def product_norms(part):
        arrived = back.at[part, pl.ds(0, 127)]
        pltpu.make_async_copy(arrived, arrived, back_recv.at[part]).wait()

        def add(channel, carry):
            return carry + back[part, channel].astype(F32)

        zero = jnp.zeros((8, 128), F32)
        center = lax.fori_loop(0, channels, add, zero, unroll=8) * (1.0 / channels)

        def square(channel, carry):
            return carry + jnp.square(back[part, channel].astype(F32) - center)

        spread = lax.fori_loop(0, channels, square, zero, unroll=8) * (1.0 / channels)
        scale = lax.rsqrt(spread + 1e-05)

        def scaled(channel, carry):
            at = pl.ds(pl.multiple_of(channel * 8, 8), 8)
            norm_f[at, :] = (back[part, channel].astype(F32) - center) * scale
            return carry

        lax.fori_loop(0, channels, scaled, 0, unroll=8)

    right, left = (place + 1) % 4, (place + 3) % 4

    def hop(slot, g):
        whole = pl.ds(g * GROUP, GROUP)
        first = pl.ds(g * GROUP, GROUP // 2)
        second = pl.ds(g * GROUP + GROUP // 2, GROUP // 2)
        other = 1 - zone
        source, part, z, x = (
            (chan, whole, other, place),
            (chan, whole, zone, right),
            (chan, whole, zone, left),
            (other * 4 + place, whole, zone, right),
            (other * 4 + place, whole, zone, left),
            (zone * 4 + left, first, zone, right),
            (zone * 4 + right, second, zone, left),
            (other * 4 + left, first, zone, right),
            (other * 4 + right, second, zone, left),
        )[slot]
        ref = everything.at[source, part]
        return remote(ref, ref, gather_send.at[slot, g], gather_recv.at[slot, g], row, z * 4 + x)

    def relay_across(g):
        hop(0, g).wait_recv()
        hop(3, g).start()
        hop(4, g).start()
        hop(1, g).wait_recv()
        hop(5, g).start()
        hop(2, g).wait_recv()
        hop(6, g).start()

    def relay_far(g):
        hop(3, g).wait_recv()
        hop(7, g).start()
        hop(4, g).wait_recv()
        hop(8, g).start()

    def finish(g):
        at = pl.ds(g * GROUP, GROUP)
        lines = []
        for t in range(GROUP):
            line = norm_f[pl.ds(g * GROUP % 8 + t, channels, stride=8), :]
            product_norm = line.astype(BF16)
            out = dot(product_norm, mult_out_ref[...], 0, 0)
            a, b, c, d = (out[rows * k : rows * k + rows] for k in range(4))
            first = core == 0
            lines.append(
                jnp.concatenate(
                    [
                        jnp.where(first, a, c),
                        jnp.where(first, c, a),
                        jnp.where(first, b, d),
                        jnp.where(first, d, b),
                    ],
                    axis=0,
                )
            )
        update = jnp.concatenate(lines, axis=0).reshape(GROUP, columns, channels)
        after = (pair_ref[at].astype(F32) + gate_f[at] * update).astype(BF16)
        after_all[at] = after
        normed = normalize(after.astype(F32), 2).astype(BF16)
        everything[chan, at] = normed
        for slot in range(3):
            hop(slot, g).start()
        padded = jnp.concatenate([normed, pad], axis=1).reshape(GROUP * 128, channels)
        bias = dot(bias_weights, padded, 1, 1)
        for t in range(GROUP):
            to = pl.ds(pl.multiple_of((g * GROUP + t) * 8, 8), 8)
            bias_f[to, :] = bias[:, t * 128 : (t + 1) * 128]

    column, slot_of_four = row // 4, (row % 4) // 2
    high, low = down // 4, down % 4

    def bias_copy(part, high_to):
        return remote(
            bias_send.at[part],
            bias_mine.at[part, chan % 4, slot_of_four, chan // 4],
            bias_out_sem.at[part, 0],
            bias_in_sem.at[part, 0],
            (high_to * 4 + chan % 4) * 2 + core,
            column,
        )

    def stays(high_to):
        here_too = jnp.logical_and(high_to == high, chan % 4 == low)
        return jnp.logical_and(here_too, chan == column)

    def bias_out(part):
        def line(h):
            return bias_f[pl.ds(part * 64 + h, 8, stride=8), :]

        for h in range(heads - 1):
            spare = pltpu.roll(line(heads - 1), columns - piece * h, 1)
            bias_send[part, h] = jnp.where(lane < columns, line(h), spare)
        for step in range(4):
            high_to = (high + step) % 4

            @pl.when(stays(high_to))
            def _():
                pltpu.make_async_copy(
                    bias_send.at[part],
                    bias_mine.at[part, chan % 4, slot_of_four, chan // 4],
                    bias_in_sem.at[part, 0],
                ).start()

            @pl.when(jnp.logical_not(stays(high_to)))
            def _():
                bias_copy(part, high_to).start()

    def bias_hop(part, apart):
        ref = bias_mine.at[part, low]
        return remote(
            ref,
            ref,
            bias_out_sem.at[part, apart],
            bias_in_sem.at[part, apart],
            (high * 4 + (low + apart) % 4) * 2 + core,
            chan,
        )

    def bias_swap(part, apart):
        source = (low + 4 - apart) % 4
        return remote(
            bias_mine.at[part, source],
            bias_theirs.at[part, source],
            bias_swap_out.at[part, apart],
            bias_swap_in.at[part, apart],
            row + 1 - 2 * core,
            chan,
        )

    def bias_pass(part):
        arrived = bias_mine.at[part, low]
        pltpu.make_async_copy(arrived, arrived, bias_in_sem.at[part, 0]).wait()
        for apart in (2, 1, 3):
            bias_hop(part, apart).start()
        bias_swap(part, 0).start()

    def bias_collect(part):
        for apart in (1, 3, 2):
            bias_hop(part, apart).wait_recv()
            bias_swap(part, apart).start()

    alive = jnp.concatenate([valid_ref[c : c + 1, 0:columns] for c in range(8)], axis=1) > 0.5

    def bias_assemble(part):
        for apart in range(4):
            bias_swap(part, apart).wait_recv()
        for ref, side in ((bias_mine, core), (bias_theirs, 1 - core)):
            for p in range(2):
                for h in range(heads):
                    if h < heads - 1:
                        parts = [ref[part, c % 4, p, c // 4, h][:, 0:columns] for c in range(8)]
                    else:
                        parts = [
                            ref[part, c % 4, p, c // 4, k][:, columns:128]
                            for c in range(8)
                            for k in range(heads - 1)
                        ]
                    line = jnp.concatenate(parts, axis=1)
                    table[h, 2 * p + side, part * 8 : part * 8 + 8] = jnp.where(
                        alive, line * LOG2E, -1e30
                    )

    product_norms(0)
    finish(0)
    finish(1)
    bias_out(0)
    relay_across(0)
    product_norms(1)
    finish(2)
    finish(3)
    bias_out(1)
    bias_pass(0)
    relay_across(1)
    relay_far(0)
    product_norms(2)
    finish(4)
    finish(5)
    bias_out(2)
    bias_pass(1)
    bias_collect(0)
    relay_across(2)
    relay_far(1)
    bias_pass(2)
    bias_collect(1)
    bias_assemble(0)
    relay_across(3)
    relay_far(2)
    bias_collect(2)
    bias_assemble(1)
    bias_assemble(2)

    keys = table.shape[3]
    head_of_lane = lax.broadcasted_iota(jnp.int32, (columns, channels), 1) // (channels // heads)
    score_scale = LOG2E / math.sqrt(channels // heads)
    ones = jnp.ones((keys, channels), BF16)

    def attend(g, carry):
        for slot in (5, 6, 7, 8):
            hop(slot, g).wait_recv()

        @pl.when(g + 4 < groups)
        def _():
            relay_across(g + 4)

        @pl.when(g + 3 < groups)
        def _():
            relay_far(g + 3)

        at = pl.ds(g * GROUP, GROUP)
        key_value = jnp.concatenate([key_ref[...], value_ref[...]], axis=1)
        for t in range(GROUP):
            i = g * GROUP + t
            tokens = jnp.concatenate([everything[c, i] for c in range(8)], axis=0)
            projected = dot(tokens, key_value).astype(BF16)
            key, value = projected[:, 0:channels], projected[:, channels:]
            query = dot(everything[chan, i], query_ref[...])
            split = jnp.concatenate(
                [jnp.where(head_of_lane == h, query, 0.0) for h in range(heads)], axis=0
            ).astype(BF16)
            score = dot(split, key, 1, 1) * score_scale + table[...].reshape(heads * columns, keys)
            raised = jnp.exp2(score - jnp.max(score, axis=1, keepdims=True)).astype(BF16)
            summed = dot(raised, jnp.concatenate([value, ones], axis=1))
            top = jnp.zeros((columns, channels), F32)
            bottom = jnp.ones((columns, channels), F32)
            for h in range(heads):
                mine_h = slice(h * columns, (h + 1) * columns)
                top = jnp.where(head_of_lane == h, summed[mine_h, 0:channels], top)
                bottom = jnp.where(head_of_lane == h, summed[mine_h, channels:], bottom)
            attended_f[pl.ds(t * columns, columns), :] = top / bottom

        normed = everything[chan, at].reshape(GROUP * columns, channels)
        gate = jax.nn.sigmoid(dot(normed, heads_gate_ref[...]))
        mixed = (gate * attended_f[...]).astype(BF16)
        after = after_all[at].reshape(GROUP * columns, channels).astype(F32)
        second = (after + dot(mixed, heads_out_ref[...])).astype(BF16)
        second_f = second.astype(F32)
        normed = normalize(second_f, 1).astype(BF16)
        hidden = jax.nn.silu(dot(normed, swish_ref[...])) * dot(normed, linear_ref[...])
        out = (second_f + dot(hidden.astype(BF16), project_ref[...])).astype(BF16)
        out_ref[at] = out.reshape(GROUP, columns, channels)
        return carry

    lax.fori_loop(0, groups, attend, 0)

    for part, send in enumerate((send_first, send_rest)):
        sent = send.at[pl.ds(0, 127)]
        pltpu.make_async_copy(sent, sent, edge_send.at[part]).wait()
    for phase in range(4):
        swap(phase).wait_send()
    for part in range(3):
        sent = back.at[part, pl.ds(0, 127)]
        pltpu.make_async_copy(sent, sent, back_send.at[part]).wait()
        for step in range(4):

            @pl.when(jnp.logical_not(stays((high + step) % 4)))
            def _():
                bias_copy(part, (high + step) % 4).wait_send()

        for apart in range(1, 4):
            bias_hop(part, apart).wait_send()
        for apart in range(4):
            bias_swap(part, apart).wait_send()

    def gather_wait(g, carry):
        for slot in range(9):
            hop(slot, g).wait_send()
        return carry

    lax.fori_loop(0, groups, gather_wait, 0)


def body(
    pair_input,
    token_valid,
    left_proj,
    left_gate,
    right_proj,
    right_gate,
    mult_gate,
    mult_out,
    query_weight,
    key_weight,
    value_weight,
    bias_weight,
    heads_gate,
    heads_out,
    swish_in,
    linear_in,
    project_out,
):
    rows, columns, channels = pair_input.shape
    heads = bias_weight.shape[1]
    tokens = token_valid.shape[0]
    valid = jnp.pad(
        token_valid.astype(F32).reshape(tokens // columns, columns), ((0, 0), (0, 128 - columns))
    )
    groups = rows // GROUP
    return pl.pallas_call(
        block_kernel,
        out_shape=jax.ShapeDtypeStruct((rows, columns, channels), BF16),
        in_specs=[VMEM, pl.BlockSpec(memory_space=pltpu.SMEM)] + [VMEM] * 16,
        out_specs=VMEM,
        scratch_shapes=[
            pltpu.VMEM((rows * channels, 128), F32),
            pltpu.VMEM((rows * channels, 128), F32),
            pltpu.VMEM((rows, columns, channels), BF16),
            pltpu.VMEM((128, rows, 128), BF16),
            pltpu.VMEM((128, 16, 128), BF16),
            pltpu.VMEM((4, 32, rows, 128), BF16),
            pltpu.VMEM((4, 32, 16, 128), BF16),
            pltpu.VMEM((4, 32, rows, 128), BF16),
            pltpu.VMEM((128, 1024), BF16),
            pltpu.VMEM((256, 1024), BF16),
            pltpu.VMEM((8, 128, 1024), BF16),
            pltpu.VMEM((3, 8, 16, 8, 128), BF16),
            pltpu.VMEM((3, 128, 8, 128), BF16),
            pltpu.VMEM((rows, columns, channels), F32),
            pltpu.VMEM((channels * 8, 128), F32),
            pltpu.VMEM((rows, columns, channels), BF16),
            pltpu.VMEM((8, rows, columns, channels), BF16),
            pltpu.VMEM((rows * 8, 128), F32),
            pltpu.VMEM((3, heads - 1, 8, 128), F32),
            pltpu.VMEM((3, 4, 2, 2, heads - 1, 8, 128), F32),
            pltpu.VMEM((3, 4, 2, 2, heads - 1, 8, 128), F32),
            pltpu.VMEM((heads, 4, rows, tokens), F32),
            pltpu.VMEM((GROUP * columns, channels), F32),
            pltpu.SemaphoreType.REGULAR,
            pltpu.SemaphoreType.DMA((2,)),
            pltpu.SemaphoreType.DMA((5,)),
            pltpu.SemaphoreType.DMA((4,)),
            pltpu.SemaphoreType.DMA((4,)),
            pltpu.SemaphoreType.DMA((3,)),
            pltpu.SemaphoreType.DMA((3,)),
            pltpu.SemaphoreType.DMA((9, groups)),
            pltpu.SemaphoreType.DMA((9, groups)),
            pltpu.SemaphoreType.DMA((3, 4)),
            pltpu.SemaphoreType.DMA((3, 4)),
            pltpu.SemaphoreType.DMA((3, 4)),
            pltpu.SemaphoreType.DMA((3, 4)),
        ],
        compiler_params=pltpu.CompilerParams(
            collective_id=0, has_side_effects=True, vmem_limit_bytes=LIMIT
        ),
        name="block",
    )(
        pair_input,
        token_valid,
        valid,
        left_proj,
        left_gate,
        right_proj,
        right_gate,
        mult_gate,
        mult_out,
        query_weight,
        key_weight,
        value_weight,
        bias_weight.T,
        heads_gate,
        heads_out,
        swish_in,
        linear_in,
        project_out,
    )


def solution(mesh):
    return jax.shard_map(
        body,
        mesh=mesh,
        in_specs=(P("row", "chan", None),) + (P(),) * 16,
        out_specs=P("row", "chan", None),
        check_vma=False,
    )
```

```python
import math

import jax
import jax.numpy as jnp
from jax import lax
from jax.experimental import pallas as pl
from jax.experimental.pallas import tpu as pltpu
from jax.sharding import PartitionSpec as P

BF16 = jnp.bfloat16
F32 = jnp.float32
LOG2E = math.log2(math.e)
MESH = pl.DeviceIdType.MESH
VMEM = pl.BlockSpec(memory_space=pltpu.VMEM)
LIMIT = 60 * 1024 * 1024
GROUP = 4


def normalize(values, axis):
    center = jnp.mean(values, axis=axis, keepdims=True)
    spread = jnp.mean(jnp.square(values - center), axis=axis, keepdims=True)
    return (values - center) * lax.rsqrt(spread + 1e-05)


def dot(a, b, a_dim=1, b_dim=0):
    return lax.dot_general(a, b, (((a_dim,), (b_dim,)), ((), ())), preferred_element_type=F32)


def transposed(ref):
    return ref[...].astype(F32).T.astype(BF16)


def remote(src, dst, send_sem, recv_sem, row, chan):
    return pltpu.make_async_remote_copy(
        src_ref=src,
        dst_ref=dst,
        send_sem=send_sem,
        recv_sem=recv_sem,
        device_id=(row, chan),
        device_id_type=MESH,
    )


def block_kernel(
    pair_ref,
    token_ref,
    valid_ref,
    left_proj_ref,
    left_gate_ref,
    right_proj_ref,
    right_gate_ref,
    mult_gate_ref,
    mult_out_ref,
    query_ref,
    key_ref,
    value_ref,
    bias_weight_ref,
    heads_gate_ref,
    heads_out_ref,
    swish_ref,
    linear_ref,
    project_ref,
    out_ref,
    left_f,
    right_f,
    normed0,
    send_first,
    send_rest,
    mine_first,
    mine_rest,
    theirs,
    left_first,
    left_rest,
    right_all,
    product,
    back,
    gate_f,
    norm_f,
    after_all,
    everything,
    bias_f,
    bias_send,
    bias_mine,
    bias_theirs,
    table,
    attended_f,
    met_sem,
    edge_send,
    edge_recv,
    swap_send,
    swap_recv,
    back_send,
    back_recv,
    gather_send,
    gather_recv,
    bias_out_sem,
    bias_in_sem,
    bias_swap_out,
    bias_swap_in,
):
    rows, columns, channels = pair_ref.shape
    groups = rows // GROUP
    heads = bias_weight_ref.shape[0]
    row, chan = lax.axis_index("row"), lax.axis_index("chan")
    core, down = row % 2, row // 2
    zone, place = chan // 4, chan % 4
    here = down * 8 + chan
    pad = jnp.zeros((GROUP, 128 - columns, channels), BF16)

    def chip(step):
        dx, dz, dd = step // 32, (step // 16) % 2, step % 16
        return (down + dd) % 16, (zone + dz) % 2, (place + dx) % 4

    barrier = pltpu.get_barrier_semaphore()

    def signal(sem, d, c, r):
        pl.semaphore_signal(sem, inc=1, device_id=(d * 2 + r, c), device_id_type=MESH)

    signal(barrier, down, chan, 1 - core)
    for step in range(1, 16):
        signal(barrier, (down + step) % 16, chan, core)
    for step in range(1, 8):
        signal(barrier, down, (chan + step) % 8, core)

    weights = jnp.concatenate(
        [transposed(ref) for ref in (left_gate_ref, left_proj_ref, right_gate_ref, right_proj_ref)],
        axis=0,
    )

    valid = jnp.broadcast_to(valid_ref[...].reshape(1, 768).astype(F32), (8, 768))
    column_mask = pltpu.roll(valid, (768 - columns * chan) % 768, 1)[0:1, 0:128]

    def edges(g, carry):
        at = pl.ds(g * GROUP, GROUP)
        normed = normalize(pair_ref[at].astype(F32), 2).astype(BF16)
        normed0[at] = normed
        padded = jnp.concatenate([normed, pad], axis=1).reshape(GROUP * 128, channels)
        out = dot(weights, padded, 1, 1)
        for t in range(GROUP):
            lanes = slice(t * 128, (t + 1) * 128)
            mask = column_mask * token_ref[row * rows + g * GROUP + t].astype(F32)
            to = pl.ds(pl.multiple_of((g * GROUP + t) * channels, channels), channels)
            left_f[to, :] = mask * jax.nn.sigmoid(out[0:128, lanes]) * out[128:256, lanes]
            right_f[to, :] = mask * jax.nn.sigmoid(out[256:384, lanes]) * out[384:512, lanes]
        return carry

    lax.fori_loop(0, groups, edges, 0)
    pl.semaphore_wait(barrier, 23)
    for step in range(1, 8):
        signal(met_sem, down, (chan + step) % 8, core)

    lane = lax.broadcasted_iota(jnp.int32, (8, 128), 1)
    piece = 128 - columns

    def edge_blocks(channel):
        at = pl.ds(channel, rows, stride=channels)
        right, left = right_f[at, :], left_f[at, :]
        packed = [
            jnp.where(
                lane < columns,
                right[8 * k : 8 * k + 8],
                pltpu.roll(left[0:8], columns - piece * k, 1),
            )
            for k in range(3)
        ]
        return jnp.concatenate(packed, axis=0).astype(BF16), left[8:rows].astype(BF16)

    def edge_copy(step, part):
        d, z, x = chip(step)
        channel = d * 8 + z * 4 + x
        send, mine = ((send_first, mine_first), (send_rest, mine_rest))[part]
        return remote(
            send.at[channel],
            mine.at[place, zone * 16 + down],
            edge_send.at[part],
            edge_recv.at[step // 32 if part == 0 else 4],
            d * 2 + core,
            z * 4 + x,
        )

    def edge_out(step, carry):
        d, z, x = chip(step)
        channel = d * 8 + z * 4 + x
        send_first[channel], send_rest[channel] = edge_blocks(channel)
        edge_copy(step, 0).start()
        return carry

    lax.fori_loop(1, 16, edge_out, 0)
    pl.semaphore_wait(met_sem, 7)
    lax.fori_loop(16, 128, edge_out, 0)
    mine_first[place, zone * 16 + down], mine_rest[place, zone * 16 + down] = edge_blocks(here)
    lax.fori_loop(1, 128, lambda step, carry: (edge_copy(step, 1).start(), carry)[1], 0)

    def gates(g, carry):
        at = pl.ds(g * GROUP, GROUP)
        normed = normed0[at].reshape(GROUP * columns, channels)
        gate = jax.nn.sigmoid(dot(normed, mult_gate_ref[...]))
        gate_f[at] = gate.reshape(GROUP, columns, channels)
        return carry

    lax.fori_loop(0, groups, gates, 0)

    def swap(phase):
        source = (place + 4 - phase) % 4
        return remote(
            mine_first.at[source],
            theirs.at[source],
            swap_send.at[phase],
            swap_recv.at[phase],
            row + 1 - 2 * core,
            chan,
        )

    def arrive(phase):
        arrived = mine_first.at[0, pl.ds(0, 31 if phase == 0 else 32)]
        pltpu.make_async_copy(arrived, arrived, edge_recv.at[phase]).wait()
        swap(phase).start()

    right_all[:, columns:128] = jnp.zeros((8, piece, 1024), BF16)
    lanes_of = lax.broadcasted_iota(jnp.int32, (128, 128), 1)

    def stage(phase):
        source = (place + 4 - phase) % 4
        for z in range(2):
            lanes = slice(phase * 256 + z * 128, phase * 256 + (z + 1) * 128)
            own = mine_first[source, z * 16 : (z + 1) * 16].astype(F32)
            other = theirs[source, z * 16 : (z + 1) * 16].astype(F32)
            both = jnp.concatenate([own.reshape(8, 48, 128), other.reshape(8, 48, 128)], axis=1)
            right_all[:, 0:columns, lanes] = both.astype(BF16)
            left = jnp.zeros((128, 128), F32)
            for k in range(3):
                turned = pltpu.roll(
                    own[:, 8 * k : 8 * k + 8].reshape(128, 128), piece + piece * k, 1
                )
                left = jnp.where(lanes_of // piece == k, turned, left)
            left_first[:, lanes] = left.astype(BF16)

    for phase in range(4):
        arrive(phase)
        if phase > 0:
            swap(phase - 1).wait_recv()
            stage(phase - 1)
    swap(3).wait_recv()
    stage(3)

    def back_out(part, turn):
        pair = (chan // 2 + turn) % 4

        def start(step, carry):
            d, c = (down + step // 2) % 16, pair * 2 + (chan + step) % 2

            @pl.when(d * 8 + c != here)
            def _():
                remote(
                    product.at[part, c, d],
                    back.at[part, here],
                    back_send.at[part],
                    back_recv.at[part],
                    d * 2 + core,
                    c,
                ).start()

            return carry

        lax.fori_loop(0, 32, start, 0)

    def multiply(left, first_part, turn):
        pair = (chan // 2 + turn) % 4
        right = right_all[pl.ds(pair * 2, 2)].reshape(256, 1024)
        out = dot(left[...], right, 1, 1)
        for side in range(2):
            block = out[:, side * 128 : (side + 1) * 128].reshape(16, -1, 128)
            for k in range(block.shape[1] // 8):
                product[first_part + k, pair * 2 + side] = block[:, 8 * k : 8 * k + 8].astype(BF16)
        back_out(first_part, turn)

    turns = (1, 2, 3, 0)
    for turn in turns:
        multiply(left_first, 0, turn)
    arrived = send_rest.at[pl.ds(0, 127)]
    pltpu.make_async_copy(arrived, arrived, edge_recv.at[4]).wait()
    for phase in range(4):
        source = (place + 4 - phase) % 4
        for z in range(2):
            lanes = slice(phase * 256 + z * 128, phase * 256 + (z + 1) * 128)
            left_rest[:, lanes] = mine_rest[source, z * 16 : (z + 1) * 16].reshape(256, 128)
    for turn in turns:
        multiply(left_rest, 1, turn)
    for turn in turns:
        back_out(2, turn)
    for part in range(3):
        back[part, here] = product[part, chan, down]
    bias_weights = jnp.concatenate(
        [bias_weight_ref[...].astype(F32), jnp.zeros((8 - heads, channels), F32)], axis=0
    ).astype(BF16)

    def product_norms(part):
        arrived = back.at[part, pl.ds(0, 127)]
        pltpu.make_async_copy(arrived, arrived, back_recv.at[part]).wait()

        def add(channel, carry):
            return carry + back[part, channel].astype(F32)

        zero = jnp.zeros((8, 128), F32)
        center = lax.fori_loop(0, channels, add, zero, unroll=8) * (1.0 / channels)

        def square(channel, carry):
            return carry + jnp.square(back[part, channel].astype(F32) - center)

        spread = lax.fori_loop(0, channels, square, zero, unroll=8) * (1.0 / channels)
        scale = lax.rsqrt(spread + 1e-05)

        def scaled(channel, carry):
            at = pl.ds(pl.multiple_of(channel * 8, 8), 8)
            norm_f[at, :] = (back[part, channel].astype(F32) - center) * scale
            return carry

        lax.fori_loop(0, channels, scaled, 0, unroll=8)

    right, left, opposite = (place + 1) % 4, (place + 3) % 4, (place + 2) % 4
    far_zone = 1 - zone

    def hop(slot, g):
        whole = pl.ds(g * GROUP, GROUP)
        first = pl.ds(g * GROUP, GROUP // 2)
        second = pl.ds(g * GROUP + GROUP // 2, GROUP // 2)
        source, part, z, x = (
            (chan, whole, far_zone, place),
            (chan, whole, zone, right),
            (chan, whole, zone, left),
            (far_zone * 4 + place, whole, zone, right),
            (far_zone * 4 + place, whole, zone, left),
            (zone * 4 + left, first, zone, right),
            (zone * 4 + right, second, zone, left),
            (zone * 4 + opposite, whole, far_zone, place),
        )[slot]
        ref = everything.at[source, part]
        return remote(ref, ref, gather_send.at[slot, g], gather_recv.at[slot, g], row, z * 4 + x)

    def relay(g):
        hop(0, g).wait_recv()
        hop(3, g).start()
        hop(4, g).start()
        hop(1, g).wait_recv()
        hop(5, g).start()
        hop(2, g).wait_recv()
        hop(6, g).start()

    def relay_back(g):
        hop(5, g).wait_recv()
        hop(6, g).wait_recv()
        hop(7, g).start()

    def finish(g):
        at = pl.ds(g * GROUP, GROUP)
        lines = []
        for t in range(GROUP):
            line = norm_f[pl.ds(g * GROUP % 8 + t, channels, stride=8), :]
            product_norm = line.astype(BF16)
            out = dot(product_norm, mult_out_ref[...], 0, 0)
            a, b, c, d = (out[rows * k : rows * k + rows] for k in range(4))
            first = core == 0
            lines.append(
                jnp.concatenate(
                    [
                        jnp.where(first, a, c),
                        jnp.where(first, c, a),
                        jnp.where(first, b, d),
                        jnp.where(first, d, b),
                    ],
                    axis=0,
                )
            )
        update = jnp.concatenate(lines, axis=0).reshape(GROUP, columns, channels)
        after = (pair_ref[at].astype(F32) + gate_f[at] * update).astype(BF16)
        after_all[at] = after
        normed = normalize(after.astype(F32), 2).astype(BF16)
        everything[chan, at] = normed
        for slot in range(3):
            hop(slot, g).start()
        padded = jnp.concatenate([normed, pad], axis=1).reshape(GROUP * 128, channels)
        bias = dot(bias_weights, padded, 1, 1)
        for t in range(GROUP):
            to = pl.ds(pl.multiple_of((g * GROUP + t) * 8, 8), 8)
            bias_f[to, :] = bias[:, t * 128 : (t + 1) * 128]

    column, slot_of_four = row // 4, (row % 4) // 2
    high, low = down // 4, down % 4

    def bias_copy(part, high_to):
        return remote(
            bias_send.at[part],
            bias_mine.at[part, chan % 4, slot_of_four, chan // 4],
            bias_out_sem.at[part, 0],
            bias_in_sem.at[part, 0],
            (high_to * 4 + chan % 4) * 2 + core,
            column,
        )

    def stays(high_to):
        here_too = jnp.logical_and(high_to == high, chan % 4 == low)
        return jnp.logical_and(here_too, chan == column)

    def bias_out(part):
        def line(h):
            return bias_f[pl.ds(part * 64 + h, 8, stride=8), :]

        for h in range(heads - 1):
            spare = pltpu.roll(line(heads - 1), columns - piece * h, 1)
            bias_send[part, h] = jnp.where(lane < columns, line(h), spare)
        for step in range(4):
            high_to = (high + step) % 4

            @pl.when(stays(high_to))
            def _():
                pltpu.make_async_copy(
                    bias_send.at[part],
                    bias_mine.at[part, chan % 4, slot_of_four, chan // 4],
                    bias_in_sem.at[part, 0],
                ).start()

            @pl.when(jnp.logical_not(stays(high_to)))
            def _():
                bias_copy(part, high_to).start()

    def bias_hop(part, apart):
        ref = bias_mine.at[part, low]
        return remote(
            ref,
            ref,
            bias_out_sem.at[part, apart],
            bias_in_sem.at[part, apart],
            (high * 4 + (low + apart) % 4) * 2 + core,
            chan,
        )

    def bias_swap(part, apart):
        source = (low + 4 - apart) % 4
        return remote(
            bias_mine.at[part, source],
            bias_theirs.at[part, source],
            bias_swap_out.at[part, apart],
            bias_swap_in.at[part, apart],
            row + 1 - 2 * core,
            chan,
        )

    def bias_pass(part):
        arrived = bias_mine.at[part, low]
        pltpu.make_async_copy(arrived, arrived, bias_in_sem.at[part, 0]).wait()
        for apart in (2, 1, 3):
            bias_hop(part, apart).start()
        bias_swap(part, 0).start()

    def bias_collect(part):
        for apart in (1, 3, 2):
            bias_hop(part, apart).wait_recv()
            bias_swap(part, apart).start()

    alive = valid[0:1] > 0.5

    def bias_assemble(part):
        for apart in range(4):
            bias_swap(part, apart).wait_recv()
        for ref, side in ((bias_mine, core), (bias_theirs, 1 - core)):
            for p in range(2):
                for h in range(heads):
                    if h < heads - 1:
                        parts = [ref[part, c % 4, p, c // 4, h][:, 0:columns] for c in range(8)]
                    else:
                        parts = [
                            ref[part, c % 4, p, c // 4, k][:, columns:128]
                            for c in range(8)
                            for k in range(heads - 1)
                        ]
                    line = jnp.concatenate(parts, axis=1)
                    table[h, 2 * p + side, part * 8 : part * 8 + 8] = jnp.where(
                        alive, line * LOG2E, -1e30
                    )

    product_norms(0)
    finish(0)
    finish(1)
    bias_out(0)
    relay(0)
    product_norms(1)
    finish(2)
    finish(3)
    bias_out(1)
    bias_pass(0)
    relay(1)
    product_norms(2)
    finish(4)
    finish(5)
    bias_out(2)
    bias_pass(1)
    bias_collect(0)
    relay(2)
    relay(3)
    bias_pass(2)
    bias_collect(1)
    bias_assemble(0)
    relay_back(0)
    relay(4)
    bias_collect(2)
    relay(5)
    relay_back(1)
    bias_assemble(1)
    bias_assemble(2)

    keys = table.shape[3]
    head_of_lane = lax.broadcasted_iota(jnp.int32, (columns, channels), 1) // (channels // heads)
    score_scale = LOG2E / math.sqrt(channels // heads)
    ones = jnp.ones((keys, channels), BF16)

    def attend(g, carry):
        for slot in (3, 4, 7):
            hop(slot, g).wait_recv()

        @pl.when(g + 2 < groups)
        def _():
            relay_back(g + 2)

        at = pl.ds(g * GROUP, GROUP)
        key_value = jnp.concatenate([key_ref[...], value_ref[...]], axis=1)
        for t in range(GROUP):
            i = g * GROUP + t
            tokens = jnp.concatenate([everything[c, i] for c in range(8)], axis=0)
            projected = dot(tokens, key_value).astype(BF16)
            key, value = projected[:, 0:channels], projected[:, channels:]
            query = dot(everything[chan, i], query_ref[...])
            split = jnp.concatenate(
                [jnp.where(head_of_lane == h, query, 0.0) for h in range(heads)], axis=0
            ).astype(BF16)
            score = dot(split, key, 1, 1) * score_scale + table[...].reshape(heads * columns, keys)
            raised = jnp.exp2(score - jnp.max(score, axis=1, keepdims=True)).astype(BF16)
            summed = dot(raised, jnp.concatenate([value, ones], axis=1))
            top = jnp.zeros((columns, channels), F32)
            bottom = jnp.ones((columns, channels), F32)
            for h in range(heads):
                mine_h = slice(h * columns, (h + 1) * columns)
                top = jnp.where(head_of_lane == h, summed[mine_h, 0:channels], top)
                bottom = jnp.where(head_of_lane == h, summed[mine_h, channels:], bottom)
            attended_f[pl.ds(t * columns, columns), :] = top / bottom

        normed = everything[chan, at].reshape(GROUP * columns, channels)
        gate = jax.nn.sigmoid(dot(normed, heads_gate_ref[...]))
        mixed = (gate * attended_f[...]).astype(BF16)
        after = after_all[at].reshape(GROUP * columns, channels).astype(F32)
        second = (after + dot(mixed, heads_out_ref[...])).astype(BF16)
        second_f = second.astype(F32)
        normed = normalize(second_f, 1).astype(BF16)
        hidden = jax.nn.silu(dot(normed, swish_ref[...])) * dot(normed, linear_ref[...])
        out = (second_f + dot(hidden.astype(BF16), project_ref[...])).astype(BF16)
        out_ref[at] = out.reshape(GROUP, columns, channels)
        return carry

    lax.fori_loop(0, groups, attend, 0)

    for part, send in enumerate((send_first, send_rest)):
        sent = send.at[pl.ds(0, 127)]
        pltpu.make_async_copy(sent, sent, edge_send.at[part]).wait()
    for phase in range(4):
        swap(phase).wait_send()
    for part in range(3):
        sent = back.at[part, pl.ds(0, 127)]
        pltpu.make_async_copy(sent, sent, back_send.at[part]).wait()
        for step in range(4):

            @pl.when(jnp.logical_not(stays((high + step) % 4)))
            def _():
                bias_copy(part, (high + step) % 4).wait_send()

        for apart in range(1, 4):
            bias_hop(part, apart).wait_send()
        for apart in range(4):
            bias_swap(part, apart).wait_send()

    def gather_wait(g, carry):
        for slot in range(8):
            hop(slot, g).wait_send()
        return carry

    lax.fori_loop(0, groups, gather_wait, 0)


def body(
    pair_input,
    token_valid,
    left_proj,
    left_gate,
    right_proj,
    right_gate,
    mult_gate,
    mult_out,
    query_weight,
    key_weight,
    value_weight,
    bias_weight,
    heads_gate,
    heads_out,
    swish_in,
    linear_in,
    project_out,
):
    rows, columns, channels = pair_input.shape
    heads = bias_weight.shape[1]
    tokens = token_valid.shape[0]
    groups = rows // GROUP
    return pl.pallas_call(
        block_kernel,
        out_shape=jax.ShapeDtypeStruct((rows, columns, channels), BF16),
        in_specs=[VMEM, pl.BlockSpec(memory_space=pltpu.SMEM)] + [VMEM] * 16,
        out_specs=VMEM,
        scratch_shapes=[
            pltpu.VMEM((rows * channels, 128), F32),
            pltpu.VMEM((rows * channels, 128), F32),
            pltpu.VMEM((rows, columns, channels), BF16),
            pltpu.VMEM((128, rows, 128), BF16),
            pltpu.VMEM((128, 16, 128), BF16),
            pltpu.VMEM((4, 32, rows, 128), BF16),
            pltpu.VMEM((4, 32, 16, 128), BF16),
            pltpu.VMEM((4, 32, rows, 128), BF16),
            pltpu.VMEM((128, 1024), BF16),
            pltpu.VMEM((256, 1024), BF16),
            pltpu.VMEM((8, 128, 1024), BF16),
            pltpu.VMEM((3, 8, 16, 8, 128), BF16),
            pltpu.VMEM((3, 128, 8, 128), BF16),
            pltpu.VMEM((rows, columns, channels), F32),
            pltpu.VMEM((channels * 8, 128), F32),
            pltpu.VMEM((rows, columns, channels), BF16),
            pltpu.VMEM((8, rows, columns, channels), BF16),
            pltpu.VMEM((rows * 8, 128), F32),
            pltpu.VMEM((3, heads - 1, 8, 128), F32),
            pltpu.VMEM((3, 4, 2, 2, heads - 1, 8, 128), F32),
            pltpu.VMEM((3, 4, 2, 2, heads - 1, 8, 128), F32),
            pltpu.VMEM((heads, 4, rows, tokens), F32),
            pltpu.VMEM((GROUP * columns, channels), F32),
            pltpu.SemaphoreType.REGULAR,
            pltpu.SemaphoreType.DMA((2,)),
            pltpu.SemaphoreType.DMA((5,)),
            pltpu.SemaphoreType.DMA((4,)),
            pltpu.SemaphoreType.DMA((4,)),
            pltpu.SemaphoreType.DMA((3,)),
            pltpu.SemaphoreType.DMA((3,)),
            pltpu.SemaphoreType.DMA((8, groups)),
            pltpu.SemaphoreType.DMA((8, groups)),
            pltpu.SemaphoreType.DMA((3, 4)),
            pltpu.SemaphoreType.DMA((3, 4)),
            pltpu.SemaphoreType.DMA((3, 4)),
            pltpu.SemaphoreType.DMA((3, 4)),
        ],
        compiler_params=pltpu.CompilerParams(
            collective_id=0, has_side_effects=True, vmem_limit_bytes=LIMIT
        ),
        name="block",
    )(
        pair_input,
        token_valid,
        token_valid,
        left_proj,
        left_gate,
        right_proj,
        right_gate,
        mult_gate,
        mult_out,
        query_weight,
        key_weight,
        value_weight,
        bias_weight.T,
        heads_gate,
        heads_out,
        swish_in,
        linear_in,
        project_out,
    )


def solution(mesh):
    return jax.shard_map(
        body,
        mesh=mesh,
        in_specs=(P("row", "chan", None),) + (P(),) * 16,
        out_specs=P("row", "chan", None),
        check_vma=False,
    )
```

```python
import math

import jax
import jax.numpy as jnp
from jax import lax
from jax.experimental import pallas as pl
from jax.experimental.pallas import tpu as pltpu
from jax.sharding import PartitionSpec as P

BF16 = jnp.bfloat16
F32 = jnp.float32
LOG2E = math.log2(math.e)
MESH = pl.DeviceIdType.MESH
VMEM = pl.BlockSpec(memory_space=pltpu.VMEM)
LIMIT = 60 * 1024 * 1024
GROUP = 4


def normalize(values, axis):
    center = jnp.mean(values, axis=axis, keepdims=True)
    spread = jnp.mean(jnp.square(values - center), axis=axis, keepdims=True)
    return (values - center) * lax.rsqrt(spread + 1e-05)


def dot(a, b, a_dim=1, b_dim=0):
    return lax.dot_general(a, b, (((a_dim,), (b_dim,)), ((), ())), preferred_element_type=F32)


def transposed(ref):
    return ref[...].astype(F32).T.astype(BF16)


def remote(src, dst, send_sem, recv_sem, row, chan):
    return pltpu.make_async_remote_copy(
        src_ref=src,
        dst_ref=dst,
        send_sem=send_sem,
        recv_sem=recv_sem,
        device_id=(row, chan),
        device_id_type=MESH,
    )


def block_kernel(
    pair_ref,
    token_ref,
    valid_ref,
    left_proj_ref,
    left_gate_ref,
    right_proj_ref,
    right_gate_ref,
    mult_gate_ref,
    mult_out_ref,
    query_ref,
    key_ref,
    value_ref,
    bias_weight_ref,
    heads_gate_ref,
    heads_out_ref,
    swish_ref,
    linear_ref,
    project_ref,
    out_ref,
    left_f,
    right_f,
    normed0,
    send_first,
    send_rest,
    mine_first,
    mine_rest,
    theirs,
    left_first,
    left_rest,
    right_all,
    product,
    back,
    gate_f,
    norm_f,
    after_all,
    everything,
    bias_f,
    bias_send,
    bias_mine,
    bias_theirs,
    table,
    attended_f,
    met_sem,
    edge_send,
    edge_recv,
    swap_send,
    swap_recv,
    back_send,
    back_recv,
    gather_send,
    gather_recv,
    bias_out_sem,
    bias_in_sem,
    bias_swap_out,
    bias_swap_in,
):
    rows, columns, channels = pair_ref.shape
    groups = rows // GROUP
    heads = bias_weight_ref.shape[0]
    row, chan = lax.axis_index("row"), lax.axis_index("chan")
    core, down = row % 2, row // 2
    zone, place = chan // 4, chan % 4
    here = down * 8 + chan
    pad = jnp.zeros((GROUP, 128 - columns, channels), BF16)

    def chip(step):
        dx, dz, dd = step // 32, (step // 16) % 2, step % 16
        return (down + dd) % 16, (zone + dz) % 2, (place + dx) % 4

    barrier = pltpu.get_barrier_semaphore()

    def signal(sem, d, c, r):
        pl.semaphore_signal(sem, inc=1, device_id=(d * 2 + r, c), device_id_type=MESH)

    signal(barrier, down, chan, 1 - core)
    for step in range(1, 16):
        signal(barrier, (down + step) % 16, chan, core)
    for step in range(1, 8):
        signal(barrier, down, (chan + step) % 8, core)

    weights = jnp.concatenate(
        [transposed(ref) for ref in (left_gate_ref, left_proj_ref, right_gate_ref, right_proj_ref)],
        axis=0,
    )

    valid = jnp.broadcast_to(valid_ref[...].reshape(1, 768).astype(F32), (8, 768))
    column_mask = pltpu.roll(valid, (768 - columns * chan) % 768, 1)[0:1, 0:128]

    def edges(g, carry):
        at = pl.ds(g * GROUP, GROUP)
        normed = normalize(pair_ref[at].astype(F32), 2).astype(BF16)
        normed0[at] = normed
        padded = jnp.concatenate([normed, pad], axis=1).reshape(GROUP * 128, channels)
        out = dot(weights, padded, 1, 1)
        for t in range(GROUP):
            lanes = slice(t * 128, (t + 1) * 128)
            mask = column_mask * token_ref[row * rows + g * GROUP + t].astype(F32)
            to = pl.ds(pl.multiple_of((g * GROUP + t) * channels, channels), channels)
            left_f[to, :] = mask * jax.nn.sigmoid(out[0:128, lanes]) * out[128:256, lanes]
            right_f[to, :] = mask * jax.nn.sigmoid(out[256:384, lanes]) * out[384:512, lanes]
        return carry

    lax.fori_loop(0, groups, edges, 0)
    pl.semaphore_wait(barrier, 23)
    for step in range(1, 8):
        signal(met_sem, down, (chan + step) % 8, core)

    lane = lax.broadcasted_iota(jnp.int32, (8, 128), 1)
    piece = 128 - columns

    def edge_blocks(channel):
        at = pl.ds(channel, rows, stride=channels)
        right, left = right_f[at, :], left_f[at, :]
        packed = [
            jnp.where(
                lane < columns,
                right[8 * k : 8 * k + 8],
                pltpu.roll(left[0:8], columns - piece * k, 1),
            )
            for k in range(3)
        ]
        return jnp.concatenate(packed, axis=0).astype(BF16), left[8:rows].astype(BF16)

    def edge_copy(step, part):
        d, z, x = chip(step)
        channel = d * 8 + z * 4 + x
        send, mine = ((send_first, mine_first), (send_rest, mine_rest))[part]
        return remote(
            send.at[channel],
            mine.at[place, zone * 16 + down],
            edge_send.at[part],
            edge_recv.at[step // 32 if part == 0 else 4],
            d * 2 + core,
            z * 4 + x,
        )

    def edge_out(step, carry):
        d, z, x = chip(step)
        channel = d * 8 + z * 4 + x
        send_first[channel], send_rest[channel] = edge_blocks(channel)
        edge_copy(step, 0).start()
        return carry

    lax.fori_loop(1, 16, edge_out, 0)
    pl.semaphore_wait(met_sem, 7)
    lax.fori_loop(16, 128, edge_out, 0)
    mine_first[place, zone * 16 + down], mine_rest[place, zone * 16 + down] = edge_blocks(here)
    lax.fori_loop(1, 128, lambda step, carry: (edge_copy(step, 1).start(), carry)[1], 0)

    def gates(g, carry):
        at = pl.ds(g * GROUP, GROUP)
        normed = normed0[at].reshape(GROUP * columns, channels)
        gate = jax.nn.sigmoid(dot(normed, mult_gate_ref[...]))
        gate_f[at] = gate.reshape(GROUP, columns, channels)
        return carry

    lax.fori_loop(0, groups, gates, 0)

    def swap(phase):
        source = (place + 4 - phase) % 4
        return remote(
            mine_first.at[source],
            theirs.at[source],
            swap_send.at[phase],
            swap_recv.at[phase],
            row + 1 - 2 * core,
            chan,
        )

    def arrive(phase):
        arrived = mine_first.at[0, pl.ds(0, 31 if phase == 0 else 32)]
        pltpu.make_async_copy(arrived, arrived, edge_recv.at[phase]).wait()
        swap(phase).start()

    right_all[:, columns:128] = jnp.zeros((8, piece, 1024), BF16)
    lanes_of = lax.broadcasted_iota(jnp.int32, (128, 128), 1)

    def stage(phase):
        source = (place + 4 - phase) % 4
        for z in range(2):
            lanes = slice(phase * 256 + z * 128, phase * 256 + (z + 1) * 128)
            own = mine_first[source, z * 16 : (z + 1) * 16].astype(F32)
            other = theirs[source, z * 16 : (z + 1) * 16].astype(F32)
            both = jnp.concatenate([own.reshape(8, 48, 128), other.reshape(8, 48, 128)], axis=1)
            right_all[:, 0:columns, lanes] = both.astype(BF16)
            left = jnp.zeros((128, 128), F32)
            for k in range(3):
                turned = pltpu.roll(
                    own[:, 8 * k : 8 * k + 8].reshape(128, 128), piece + piece * k, 1
                )
                left = jnp.where(lanes_of // piece == k, turned, left)
            left_first[:, lanes] = left.astype(BF16)

    for phase in range(4):
        arrive(phase)
        if phase > 0:
            swap(phase - 1).wait_recv()
            stage(phase - 1)
    swap(3).wait_recv()
    stage(3)

    def back_out(part, turn):
        pair = (chan // 2 + turn) % 4

        def start(step, carry):
            d, c = (down + step // 2) % 16, pair * 2 + (chan + step) % 2

            @pl.when(d * 8 + c != here)
            def _():
                remote(
                    product.at[part, c, d],
                    back.at[part, here],
                    back_send.at[part],
                    back_recv.at[part],
                    d * 2 + core,
                    c,
                ).start()

            return carry

        lax.fori_loop(0, 32, start, 0)

    def multiply(left, first_part, turn):
        pair = (chan // 2 + turn) % 4
        right = right_all[pl.ds(pair * 2, 2)].reshape(256, 1024)
        out = dot(left[...], right, 1, 1)
        for side in range(2):
            block = out[:, side * 128 : (side + 1) * 128].reshape(16, -1, 128)
            for k in range(block.shape[1] // 8):
                product[first_part + k, pair * 2 + side] = block[:, 8 * k : 8 * k + 8].astype(BF16)
        back_out(first_part, turn)

    turns = (1, 2, 3, 0)
    for turn in turns:
        multiply(left_first, 0, turn)
    arrived = send_rest.at[pl.ds(0, 127)]
    pltpu.make_async_copy(arrived, arrived, edge_recv.at[4]).wait()
    for phase in range(4):
        source = (place + 4 - phase) % 4
        for z in range(2):
            lanes = slice(phase * 256 + z * 128, phase * 256 + (z + 1) * 128)
            left_rest[:, lanes] = mine_rest[source, z * 16 : (z + 1) * 16].reshape(256, 128)
    for turn in turns:
        multiply(left_rest, 1, turn)
    for turn in turns:
        back_out(2, turn)
    for part in range(3):
        back[part, here] = product[part, chan, down]
    bias_weights = jnp.concatenate(
        [bias_weight_ref[...].astype(F32), jnp.zeros((8 - heads, channels), F32)], axis=0
    ).astype(BF16)

    def product_norms(part):
        arrived = back.at[part, pl.ds(0, 127)]
        pltpu.make_async_copy(arrived, arrived, back_recv.at[part]).wait()

        def add(channel, carry):
            return carry + back[part, channel].astype(F32)

        zero = jnp.zeros((8, 128), F32)
        center = lax.fori_loop(0, channels, add, zero, unroll=8) * (1.0 / channels)

        def square(channel, carry):
            return carry + jnp.square(back[part, channel].astype(F32) - center)

        spread = lax.fori_loop(0, channels, square, zero, unroll=8) * (1.0 / channels)
        scale = lax.rsqrt(spread + 1e-05)

        def scaled(channel, carry):
            at = pl.ds(pl.multiple_of(channel * 8, 8), 8)
            norm_f[at, :] = (back[part, channel].astype(F32) - center) * scale
            return carry

        lax.fori_loop(0, channels, scaled, 0, unroll=8)

    right, left, opposite = (place + 1) % 4, (place + 3) % 4, (place + 2) % 4
    far_zone = 1 - zone

    def hop(slot, g):
        whole = pl.ds(g * GROUP, GROUP)
        first = pl.ds(g * GROUP, GROUP // 2)
        second = pl.ds(g * GROUP + GROUP // 2, GROUP // 2)
        source, part, z, x = (
            (chan, whole, far_zone, place),
            (chan, whole, zone, right),
            (chan, whole, zone, left),
            (far_zone * 4 + place, whole, zone, right),
            (far_zone * 4 + place, whole, zone, left),
            (zone * 4 + left, first, zone, right),
            (zone * 4 + right, second, zone, left),
            (zone * 4 + opposite, whole, far_zone, place),
        )[slot]
        ref = everything.at[source, part]
        return remote(ref, ref, gather_send.at[slot, g], gather_recv.at[slot, g], row, z * 4 + x)

    def launch(g):
        for slot in range(3):
            hop(slot, g).start()

    def relay_zone(g):
        hop(0, g).wait_recv()
        hop(3, g).start()
        hop(4, g).start()

    def relay_ring(g):
        hop(1, g).wait_recv()
        hop(5, g).start()
        hop(2, g).wait_recv()
        hop(6, g).start()

    def relay_back(g):
        hop(5, g).wait_recv()
        hop(6, g).wait_recv()
        hop(7, g).start()

    def finish(g):
        at = pl.ds(g * GROUP, GROUP)
        lines = []
        for t in range(GROUP):
            line = norm_f[pl.ds(g * GROUP % 8 + t, channels, stride=8), :]
            product_norm = line.astype(BF16)
            out = dot(product_norm, mult_out_ref[...], 0, 0)
            a, b, c, d = (out[rows * k : rows * k + rows] for k in range(4))
            first = core == 0
            lines.append(
                jnp.concatenate(
                    [
                        jnp.where(first, a, c),
                        jnp.where(first, c, a),
                        jnp.where(first, b, d),
                        jnp.where(first, d, b),
                    ],
                    axis=0,
                )
            )
        update = jnp.concatenate(lines, axis=0).reshape(GROUP, columns, channels)
        after = (pair_ref[at].astype(F32) + gate_f[at] * update).astype(BF16)
        after_all[at] = after
        normed = normalize(after.astype(F32), 2).astype(BF16)
        everything[chan, at] = normed
        padded = jnp.concatenate([normed, pad], axis=1).reshape(GROUP * 128, channels)
        bias = dot(bias_weights, padded, 1, 1)
        for t in range(GROUP):
            to = pl.ds(pl.multiple_of((g * GROUP + t) * 8, 8), 8)
            bias_f[to, :] = bias[:, t * 128 : (t + 1) * 128]

    column, slot_of_four = row // 4, (row % 4) // 2
    high, low = down // 4, down % 4

    def bias_copy(part, high_to):
        return remote(
            bias_send.at[part],
            bias_mine.at[part, chan % 4, slot_of_four, chan // 4],
            bias_out_sem.at[part, 0],
            bias_in_sem.at[part, 0],
            (high_to * 4 + chan % 4) * 2 + core,
            column,
        )

    def stays(high_to):
        here_too = jnp.logical_and(high_to == high, chan % 4 == low)
        return jnp.logical_and(here_too, chan == column)

    def bias_out(part):
        def line(h):
            return bias_f[pl.ds(part * 64 + h, 8, stride=8), :]

        for h in range(heads - 1):
            spare = pltpu.roll(line(heads - 1), columns - piece * h, 1)
            bias_send[part, h] = jnp.where(lane < columns, line(h), spare)
        for step in range(4):
            high_to = (high + step) % 4

            @pl.when(stays(high_to))
            def _():
                pltpu.make_async_copy(
                    bias_send.at[part],
                    bias_mine.at[part, chan % 4, slot_of_four, chan // 4],
                    bias_in_sem.at[part, 0],
                ).start()

            @pl.when(jnp.logical_not(stays(high_to)))
            def _():
                bias_copy(part, high_to).start()

    def bias_hop(part, apart):
        ref = bias_mine.at[part, low]
        return remote(
            ref,
            ref,
            bias_out_sem.at[part, apart],
            bias_in_sem.at[part, apart],
            (high * 4 + (low + apart) % 4) * 2 + core,
            chan,
        )

    def bias_swap(part, apart):
        source = (low + 4 - apart) % 4
        return remote(
            bias_mine.at[part, source],
            bias_theirs.at[part, source],
            bias_swap_out.at[part, apart],
            bias_swap_in.at[part, apart],
            row + 1 - 2 * core,
            chan,
        )

    def bias_pass(part):
        arrived = bias_mine.at[part, low]
        pltpu.make_async_copy(arrived, arrived, bias_in_sem.at[part, 0]).wait()
        for apart in (2, 1, 3):
            bias_hop(part, apart).start()
        bias_swap(part, 0).start()

    def bias_collect(part):
        for apart in (1, 3, 2):
            bias_hop(part, apart).wait_recv()
            bias_swap(part, apart).start()

    alive = valid[0:1] > 0.5

    def bias_assemble(part):
        for apart in range(4):
            bias_swap(part, apart).wait_recv()
        for ref, side in ((bias_mine, core), (bias_theirs, 1 - core)):
            for p in range(2):
                for h in range(heads):
                    if h < heads - 1:
                        parts = [ref[part, c % 4, p, c // 4, h][:, 0:columns] for c in range(8)]
                    else:
                        parts = [
                            ref[part, c % 4, p, c // 4, k][:, columns:128]
                            for c in range(8)
                            for k in range(heads - 1)
                        ]
                    line = jnp.concatenate(parts, axis=1)
                    table[h, 2 * p + side, part * 8 : part * 8 + 8] = jnp.where(
                        alive, line * LOG2E, -1e30
                    )

    product_norms(0)
    finish(0)
    finish(1)
    launch(0)
    launch(1)
    bias_out(0)
    product_norms(1)
    finish(2)
    finish(3)
    launch(2)
    launch(3)
    bias_out(1)
    bias_pass(0)
    relay_ring(0)
    relay_zone(0)
    product_norms(2)
    finish(4)
    finish(5)
    bias_out(2)
    launch(4)
    launch(5)
    bias_pass(1)
    relay_zone(1)
    relay_ring(1)
    bias_collect(0)
    bias_pass(2)
    bias_collect(1)
    relay_zone(2)
    relay_ring(2)
    bias_assemble(0)
    bias_assemble(1)
    relay_back(0)
    relay_zone(3)
    bias_collect(2)
    bias_assemble(2)
    relay_ring(3)
    relay_zone(4)
    relay_back(1)

    keys = table.shape[3]
    head_of_lane = lax.broadcasted_iota(jnp.int32, (columns, channels), 1) // (channels // heads)
    score_scale = LOG2E / math.sqrt(channels // heads)
    ones = jnp.ones((keys, channels), BF16)

    def attend(g, carry):
        @pl.when(g == 0)
        def _():
            relay_zone(groups - 1)
            relay_ring(groups - 2)

        @pl.when(g == 1)
        def _():
            relay_ring(groups - 1)

        for slot in (3, 4, 7):
            hop(slot, g).wait_recv()

        @pl.when(g + 2 < groups)
        def _():
            relay_back(g + 2)

        at = pl.ds(g * GROUP, GROUP)
        key_value = jnp.concatenate([key_ref[...], value_ref[...]], axis=1)
        for t in range(GROUP):
            i = g * GROUP + t
            tokens = jnp.concatenate([everything[c, i] for c in range(8)], axis=0)
            projected = dot(tokens, key_value).astype(BF16)
            key, value = projected[:, 0:channels], projected[:, channels:]
            query = dot(everything[chan, i], query_ref[...])
            split = jnp.concatenate(
                [jnp.where(head_of_lane == h, query, 0.0) for h in range(heads)], axis=0
            ).astype(BF16)
            score = dot(split, key, 1, 1) * score_scale + table[...].reshape(heads * columns, keys)
            raised = jnp.exp2(score - jnp.max(score, axis=1, keepdims=True)).astype(BF16)
            summed = dot(raised, jnp.concatenate([value, ones], axis=1))
            top = jnp.zeros((columns, channels), F32)
            bottom = jnp.ones((columns, channels), F32)
            for h in range(heads):
                mine_h = slice(h * columns, (h + 1) * columns)
                top = jnp.where(head_of_lane == h, summed[mine_h, 0:channels], top)
                bottom = jnp.where(head_of_lane == h, summed[mine_h, channels:], bottom)
            attended_f[pl.ds(t * columns, columns), :] = top / bottom

        normed = everything[chan, at].reshape(GROUP * columns, channels)
        gate = jax.nn.sigmoid(dot(normed, heads_gate_ref[...]))
        mixed = (gate * attended_f[...]).astype(BF16)
        after = after_all[at].reshape(GROUP * columns, channels).astype(F32)
        second = (after + dot(mixed, heads_out_ref[...])).astype(BF16)
        second_f = second.astype(F32)
        normed = normalize(second_f, 1).astype(BF16)
        hidden = jax.nn.silu(dot(normed, swish_ref[...])) * dot(normed, linear_ref[...])
        out = (second_f + dot(hidden.astype(BF16), project_ref[...])).astype(BF16)
        out_ref[at] = out.reshape(GROUP, columns, channels)
        return carry

    lax.fori_loop(0, groups, attend, 0)

    for part, send in enumerate((send_first, send_rest)):
        sent = send.at[pl.ds(0, 127)]
        pltpu.make_async_copy(sent, sent, edge_send.at[part]).wait()
    for phase in range(4):
        swap(phase).wait_send()
    for part in range(3):
        sent = back.at[part, pl.ds(0, 127)]
        pltpu.make_async_copy(sent, sent, back_send.at[part]).wait()
        for step in range(4):

            @pl.when(jnp.logical_not(stays((high + step) % 4)))
            def _():
                bias_copy(part, (high + step) % 4).wait_send()

        for apart in range(1, 4):
            bias_hop(part, apart).wait_send()
        for apart in range(4):
            bias_swap(part, apart).wait_send()

    def gather_wait(g, carry):
        for slot in range(8):
            hop(slot, g).wait_send()
        return carry

    lax.fori_loop(0, groups, gather_wait, 0)


def body(
    pair_input,
    token_valid,
    left_proj,
    left_gate,
    right_proj,
    right_gate,
    mult_gate,
    mult_out,
    query_weight,
    key_weight,
    value_weight,
    bias_weight,
    heads_gate,
    heads_out,
    swish_in,
    linear_in,
    project_out,
):
    rows, columns, channels = pair_input.shape
    heads = bias_weight.shape[1]
    tokens = token_valid.shape[0]
    groups = rows // GROUP
    return pl.pallas_call(
        block_kernel,
        out_shape=jax.ShapeDtypeStruct((rows, columns, channels), BF16),
        in_specs=[VMEM, pl.BlockSpec(memory_space=pltpu.SMEM)] + [VMEM] * 16,
        out_specs=VMEM,
        scratch_shapes=[
            pltpu.VMEM((rows * channels, 128), F32),
            pltpu.VMEM((rows * channels, 128), F32),
            pltpu.VMEM((rows, columns, channels), BF16),
            pltpu.VMEM((128, rows, 128), BF16),
            pltpu.VMEM((128, 16, 128), BF16),
            pltpu.VMEM((4, 32, rows, 128), BF16),
            pltpu.VMEM((4, 32, 16, 128), BF16),
            pltpu.VMEM((4, 32, rows, 128), BF16),
            pltpu.VMEM((128, 1024), BF16),
            pltpu.VMEM((256, 1024), BF16),
            pltpu.VMEM((8, 128, 1024), BF16),
            pltpu.VMEM((3, 8, 16, 8, 128), BF16),
            pltpu.VMEM((3, 128, 8, 128), BF16),
            pltpu.VMEM((rows, columns, channels), F32),
            pltpu.VMEM((channels * 8, 128), F32),
            pltpu.VMEM((rows, columns, channels), BF16),
            pltpu.VMEM((8, rows, columns, channels), BF16),
            pltpu.VMEM((rows * 8, 128), F32),
            pltpu.VMEM((3, heads - 1, 8, 128), F32),
            pltpu.VMEM((3, 4, 2, 2, heads - 1, 8, 128), F32),
            pltpu.VMEM((3, 4, 2, 2, heads - 1, 8, 128), F32),
            pltpu.VMEM((heads, 4, rows, tokens), F32),
            pltpu.VMEM((GROUP * columns, channels), F32),
            pltpu.SemaphoreType.REGULAR,
            pltpu.SemaphoreType.DMA((2,)),
            pltpu.SemaphoreType.DMA((5,)),
            pltpu.SemaphoreType.DMA((4,)),
            pltpu.SemaphoreType.DMA((4,)),
            pltpu.SemaphoreType.DMA((3,)),
            pltpu.SemaphoreType.DMA((3,)),
            pltpu.SemaphoreType.DMA((8, groups)),
            pltpu.SemaphoreType.DMA((8, groups)),
            pltpu.SemaphoreType.DMA((3, 4)),
            pltpu.SemaphoreType.DMA((3, 4)),
            pltpu.SemaphoreType.DMA((3, 4)),
            pltpu.SemaphoreType.DMA((3, 4)),
        ],
        compiler_params=pltpu.CompilerParams(
            collective_id=0, has_side_effects=True, vmem_limit_bytes=LIMIT
        ),
        name="block",
    )(
        pair_input,
        token_valid,
        token_valid,
        left_proj,
        left_gate,
        right_proj,
        right_gate,
        mult_gate,
        mult_out,
        query_weight,
        key_weight,
        value_weight,
        bias_weight.T,
        heads_gate,
        heads_out,
        swish_in,
        linear_in,
        project_out,
    )


def solution(mesh):
    return jax.shard_map(
        body,
        mesh=mesh,
        in_specs=(P("row", "chan", None),) + (P(),) * 16,
        out_specs=P("row", "chan", None),
        check_vma=False,
    )
```

```python
import math

import jax
import jax.numpy as jnp
from jax import lax
from jax.experimental import pallas as pl
from jax.experimental.pallas import tpu as pltpu
from jax.sharding import PartitionSpec as P

BF16 = jnp.bfloat16
F32 = jnp.float32
LOG2E = math.log2(math.e)
MESH = pl.DeviceIdType.MESH
VMEM = pl.BlockSpec(memory_space=pltpu.VMEM)
LIMIT = 60 * 1024 * 1024
GROUP = 4


def normalize(values, axis):
    center = jnp.mean(values, axis=axis, keepdims=True)
    spread = jnp.mean(jnp.square(values - center), axis=axis, keepdims=True)
    return (values - center) * lax.rsqrt(spread + 1e-05)


def dot(a, b, a_dim=1, b_dim=0):
    return lax.dot_general(a, b, (((a_dim,), (b_dim,)), ((), ())), preferred_element_type=F32)


def transposed(ref):
    return ref[...].astype(F32).T.astype(BF16)


def remote(src, dst, send_sem, recv_sem, row, chan):
    return pltpu.make_async_remote_copy(
        src_ref=src,
        dst_ref=dst,
        send_sem=send_sem,
        recv_sem=recv_sem,
        device_id=(row, chan),
        device_id_type=MESH,
    )


def block_kernel(
    pair_ref,
    token_ref,
    valid_ref,
    left_proj_ref,
    left_gate_ref,
    right_proj_ref,
    right_gate_ref,
    mult_gate_ref,
    mult_out_ref,
    query_ref,
    key_ref,
    value_ref,
    bias_weight_ref,
    heads_gate_ref,
    heads_out_ref,
    swish_ref,
    linear_ref,
    project_ref,
    out_ref,
    left_f,
    right_f,
    normed0,
    send_first,
    send_rest,
    mine_first,
    mine_rest,
    theirs,
    left_first,
    left_rest,
    right_all,
    product,
    back,
    gate_f,
    norm_f,
    after_all,
    everything,
    bias_f,
    bias_send,
    bias_mine,
    bias_theirs,
    table,
    attended_f,
    met_sem,
    edge_send,
    edge_recv,
    swap_send,
    swap_recv,
    back_send,
    back_recv,
    gather_send,
    gather_recv,
    bias_out_sem,
    bias_in_sem,
    bias_swap_out,
    bias_swap_in,
):
    rows, columns, channels = pair_ref.shape
    groups = rows // GROUP
    heads = bias_weight_ref.shape[0]
    row, chan = lax.axis_index("row"), lax.axis_index("chan")
    core, down = row % 2, row // 2
    zone, place = chan // 4, chan % 4
    here = down * 8 + chan
    pad = jnp.zeros((GROUP, 128 - columns, channels), BF16)

    def chip(step):
        dx, dz, dd = step // 32, (step // 16) % 2, step % 16
        return (down + dd) % 16, (zone + dz) % 2, (place + dx) % 4

    barrier = pltpu.get_barrier_semaphore()

    def signal(sem, d, c, r):
        pl.semaphore_signal(sem, inc=1, device_id=(d * 2 + r, c), device_id_type=MESH)

    signal(barrier, down, chan, 1 - core)
    for step in range(1, 16):
        signal(barrier, (down + step) % 16, chan, core)
    for step in range(1, 8):
        signal(barrier, down, (chan + step) % 8, core)

    weights = jnp.concatenate(
        [transposed(ref) for ref in (left_gate_ref, left_proj_ref, right_gate_ref, right_proj_ref)],
        axis=0,
    )

    valid = jnp.broadcast_to(valid_ref[...].reshape(1, 768).astype(F32), (8, 768))
    column_mask = pltpu.roll(valid, (768 - columns * chan) % 768, 1)[0:1, 0:128]

    def edges(g, carry):
        at = pl.ds(g * GROUP, GROUP)
        normed = normalize(pair_ref[at].astype(F32), 2).astype(BF16)
        normed0[at] = normed
        padded = jnp.concatenate([normed, pad], axis=1).reshape(GROUP * 128, channels)
        out = dot(weights, padded, 1, 1)
        for t in range(GROUP):
            lanes = slice(t * 128, (t + 1) * 128)
            mask = column_mask * token_ref[row * rows + g * GROUP + t].astype(F32)
            to = pl.ds(pl.multiple_of((g * GROUP + t) * channels, channels), channels)
            left_f[to, :] = mask * jax.nn.sigmoid(out[0:128, lanes]) * out[128:256, lanes]
            right_f[to, :] = mask * jax.nn.sigmoid(out[256:384, lanes]) * out[384:512, lanes]
        return carry

    lax.fori_loop(0, groups // 2, edges, 0)
    pl.semaphore_wait(barrier, 23)
    for step in range(1, 8):
        signal(met_sem, down, (chan + step) % 8, core)
    lax.fori_loop(groups // 2, groups, edges, 0)

    lane = lax.broadcasted_iota(jnp.int32, (8, 128), 1)
    piece = 128 - columns

    def edge_blocks(channel):
        at = pl.ds(channel, rows, stride=channels)
        right, left = right_f[at, :], left_f[at, :]
        packed = [
            jnp.where(
                lane < columns,
                right[8 * k : 8 * k + 8],
                pltpu.roll(left[0:8], columns - piece * k, 1),
            )
            for k in range(3)
        ]
        return jnp.concatenate(packed, axis=0).astype(BF16), left[8:rows].astype(BF16)

    def edge_copy(step, part):
        d, z, x = chip(step)
        channel = d * 8 + z * 4 + x
        send, mine = ((send_first, mine_first), (send_rest, mine_rest))[part]
        return remote(
            send.at[channel],
            mine.at[place, zone * 16 + down],
            edge_send.at[part],
            edge_recv.at[step // 32 if part == 0 else 4],
            d * 2 + core,
            z * 4 + x,
        )

    def edge_out(step, carry):
        d, z, x = chip(step)
        channel = d * 8 + z * 4 + x
        send_first[channel], send_rest[channel] = edge_blocks(channel)
        edge_copy(step, 0).start()
        return carry

    lax.fori_loop(1, 16, edge_out, 0)
    pl.semaphore_wait(met_sem, 7)
    lax.fori_loop(16, 128, edge_out, 0)
    mine_first[place, zone * 16 + down], mine_rest[place, zone * 16 + down] = edge_blocks(here)
    lax.fori_loop(1, 128, lambda step, carry: (edge_copy(step, 1).start(), carry)[1], 0)

    def gates(g, carry):
        at = pl.ds(g * GROUP, GROUP)
        normed = normed0[at].reshape(GROUP * columns, channels)
        gate = jax.nn.sigmoid(dot(normed, mult_gate_ref[...]))
        gate_f[at] = gate.reshape(GROUP, columns, channels)
        return carry

    lax.fori_loop(0, groups, gates, 0)

    def swap(phase):
        source = (place + 4 - phase) % 4
        return remote(
            mine_first.at[source],
            theirs.at[source],
            swap_send.at[phase],
            swap_recv.at[phase],
            row + 1 - 2 * core,
            chan,
        )

    def arrive(phase):
        arrived = mine_first.at[0, pl.ds(0, 31 if phase == 0 else 32)]
        pltpu.make_async_copy(arrived, arrived, edge_recv.at[phase]).wait()
        swap(phase).start()

    right_all[:, columns:128] = jnp.zeros((8, piece, 1024), BF16)
    lanes_of = lax.broadcasted_iota(jnp.int32, (128, 128), 1)

    def stage(phase):
        source = (place + 4 - phase) % 4
        for z in range(2):
            lanes = slice(phase * 256 + z * 128, phase * 256 + (z + 1) * 128)
            own = mine_first[source, z * 16 : (z + 1) * 16].astype(F32)
            other = theirs[source, z * 16 : (z + 1) * 16].astype(F32)
            both = jnp.concatenate([own.reshape(8, 48, 128), other.reshape(8, 48, 128)], axis=1)
            right_all[:, 0:columns, lanes] = both.astype(BF16)
            left = jnp.zeros((128, 128), F32)
            for k in range(3):
                turned = pltpu.roll(
                    own[:, 8 * k : 8 * k + 8].reshape(128, 128), piece + piece * k, 1
                )
                left = jnp.where(lanes_of // piece == k, turned, left)
            left_first[:, lanes] = left.astype(BF16)

    for phase in range(4):
        arrive(phase)
        if phase > 0:
            swap(phase - 1).wait_recv()
            stage(phase - 1)
    swap(3).wait_recv()
    stage(3)

    def back_out(part, turn):
        pair = (chan // 2 + turn) % 4

        def start(step, carry):
            d, c = (down + step // 2) % 16, pair * 2 + (chan + step) % 2

            @pl.when(d * 8 + c != here)
            def _():
                remote(
                    product.at[part, c, d],
                    back.at[part, here],
                    back_send.at[part],
                    back_recv.at[part],
                    d * 2 + core,
                    c,
                ).start()

            return carry

        lax.fori_loop(0, 32, start, 0)

    def multiply(left, first_part, turn):
        pair = (chan // 2 + turn) % 4
        right = right_all[pl.ds(pair * 2, 2)].reshape(256, 1024)
        out = dot(left[...], right, 1, 1)
        for side in range(2):
            block = out[:, side * 128 : (side + 1) * 128].reshape(16, -1, 128)
            for k in range(block.shape[1] // 8):
                product[first_part + k, pair * 2 + side] = block[:, 8 * k : 8 * k + 8].astype(BF16)
        back_out(first_part, turn)

    turns = (1, 2, 3, 0)
    for turn in turns:
        multiply(left_first, 0, turn)
    arrived = send_rest.at[pl.ds(0, 127)]
    pltpu.make_async_copy(arrived, arrived, edge_recv.at[4]).wait()
    for phase in range(4):
        source = (place + 4 - phase) % 4
        for z in range(2):
            lanes = slice(phase * 256 + z * 128, phase * 256 + (z + 1) * 128)
            left_rest[:, lanes] = mine_rest[source, z * 16 : (z + 1) * 16].reshape(256, 128)
    for turn in turns:
        multiply(left_rest, 1, turn)
    for turn in turns:
        back_out(2, turn)
    for part in range(3):
        back[part, here] = product[part, chan, down]
    bias_weights = jnp.concatenate(
        [bias_weight_ref[...].astype(F32), jnp.zeros((8 - heads, channels), F32)], axis=0
    ).astype(BF16)

    def product_norms(part):
        arrived = back.at[part, pl.ds(0, 127)]
        pltpu.make_async_copy(arrived, arrived, back_recv.at[part]).wait()

        def add(channel, carry):
            return carry + back[part, channel].astype(F32)

        zero = jnp.zeros((8, 128), F32)
        center = lax.fori_loop(0, channels, add, zero, unroll=8) * (1.0 / channels)

        def square(channel, carry):
            return carry + jnp.square(back[part, channel].astype(F32) - center)

        spread = lax.fori_loop(0, channels, square, zero, unroll=8) * (1.0 / channels)
        scale = lax.rsqrt(spread + 1e-05)

        def scaled(channel, carry):
            at = pl.ds(pl.multiple_of(channel * 8, 8), 8)
            norm_f[at, :] = (back[part, channel].astype(F32) - center) * scale
            return carry

        lax.fori_loop(0, channels, scaled, 0, unroll=8)

    right, left, opposite = (place + 1) % 4, (place + 3) % 4, (place + 2) % 4
    far_zone = 1 - zone

    def hop(slot, g):
        whole = pl.ds(g * GROUP, GROUP)
        first = pl.ds(g * GROUP, GROUP // 2)
        second = pl.ds(g * GROUP + GROUP // 2, GROUP // 2)
        source, part, z, x = (
            (chan, whole, far_zone, place),
            (chan, whole, zone, right),
            (chan, whole, zone, left),
            (far_zone * 4 + place, whole, zone, right),
            (far_zone * 4 + place, whole, zone, left),
            (zone * 4 + left, first, zone, right),
            (zone * 4 + right, second, zone, left),
            (zone * 4 + opposite, whole, far_zone, place),
        )[slot]
        ref = everything.at[source, part]
        return remote(ref, ref, gather_send.at[slot, g], gather_recv.at[slot, g], row, z * 4 + x)

    def launch(g):
        for slot in range(3):
            hop(slot, g).start()

    def relay_zone(g):
        hop(0, g).wait_recv()
        hop(3, g).start()
        hop(4, g).start()

    def relay_ring(g):
        hop(1, g).wait_recv()
        hop(5, g).start()
        hop(2, g).wait_recv()
        hop(6, g).start()

    def relay_back(g):
        hop(5, g).wait_recv()
        hop(6, g).wait_recv()
        hop(7, g).start()

    def finish(g):
        at = pl.ds(g * GROUP, GROUP)
        lines = []
        for t in range(GROUP):
            line = norm_f[pl.ds(g * GROUP % 8 + t, channels, stride=8), :]
            product_norm = line.astype(BF16)
            out = dot(product_norm, mult_out_ref[...], 0, 0)
            a, b, c, d = (out[rows * k : rows * k + rows] for k in range(4))
            first = core == 0
            lines.append(
                jnp.concatenate(
                    [
                        jnp.where(first, a, c),
                        jnp.where(first, c, a),
                        jnp.where(first, b, d),
                        jnp.where(first, d, b),
                    ],
                    axis=0,
                )
            )
        update = jnp.concatenate(lines, axis=0).reshape(GROUP, columns, channels)
        after = (pair_ref[at].astype(F32) + gate_f[at] * update).astype(BF16)
        after_all[at] = after
        normed = normalize(after.astype(F32), 2).astype(BF16)
        everything[chan, at] = normed
        padded = jnp.concatenate([normed, pad], axis=1).reshape(GROUP * 128, channels)
        bias = dot(bias_weights, padded, 1, 1)
        for t in range(GROUP):
            to = pl.ds(pl.multiple_of((g * GROUP + t) * 8, 8), 8)
            bias_f[to, :] = bias[:, t * 128 : (t + 1) * 128]

    column, slot_of_four = row // 4, (row % 4) // 2
    high, low = down // 4, down % 4

    def bias_copy(part, high_to):
        return remote(
            bias_send.at[part],
            bias_mine.at[part, chan % 4, slot_of_four, chan // 4],
            bias_out_sem.at[part, 0],
            bias_in_sem.at[part, 0],
            (high_to * 4 + chan % 4) * 2 + core,
            column,
        )

    def stays(high_to):
        here_too = jnp.logical_and(high_to == high, chan % 4 == low)
        return jnp.logical_and(here_too, chan == column)

    def bias_out(part):
        def line(h):
            return bias_f[pl.ds(part * 64 + h, 8, stride=8), :]

        for h in range(heads - 1):
            spare = pltpu.roll(line(heads - 1), columns - piece * h, 1)
            bias_send[part, h] = jnp.where(lane < columns, line(h), spare)
        for step in range(4):
            high_to = (high + step) % 4

            @pl.when(stays(high_to))
            def _():
                pltpu.make_async_copy(
                    bias_send.at[part],
                    bias_mine.at[part, chan % 4, slot_of_four, chan // 4],
                    bias_in_sem.at[part, 0],
                ).start()

            @pl.when(jnp.logical_not(stays(high_to)))
            def _():
                bias_copy(part, high_to).start()

    def bias_hop(part, apart):
        ref = bias_mine.at[part, low]
        return remote(
            ref,
            ref,
            bias_out_sem.at[part, apart],
            bias_in_sem.at[part, apart],
            (high * 4 + (low + apart) % 4) * 2 + core,
            chan,
        )

    def bias_swap(part, apart):
        source = (low + 4 - apart) % 4
        return remote(
            bias_mine.at[part, source],
            bias_theirs.at[part, source],
            bias_swap_out.at[part, apart],
            bias_swap_in.at[part, apart],
            row + 1 - 2 * core,
            chan,
        )

    def bias_pass(part):
        arrived = bias_mine.at[part, low]
        pltpu.make_async_copy(arrived, arrived, bias_in_sem.at[part, 0]).wait()
        for apart in (2, 1, 3):
            bias_hop(part, apart).start()
        bias_swap(part, 0).start()

    def bias_collect(part):
        for apart in (1, 3, 2):
            bias_hop(part, apart).wait_recv()
            bias_swap(part, apart).start()

    alive = valid[0:1] > 0.5

    def bias_assemble(part):
        for apart in range(4):
            bias_swap(part, apart).wait_recv()
        for ref, side in ((bias_mine, core), (bias_theirs, 1 - core)):
            for p in range(2):
                for h in range(heads):
                    if h < heads - 1:
                        parts = [ref[part, c % 4, p, c // 4, h][:, 0:columns] for c in range(8)]
                    else:
                        parts = [
                            ref[part, c % 4, p, c // 4, k][:, columns:128]
                            for c in range(8)
                            for k in range(heads - 1)
                        ]
                    line = jnp.concatenate(parts, axis=1)
                    table[h, 2 * p + side, part * 8 : part * 8 + 8] = jnp.where(
                        alive, line * LOG2E, -1e30
                    )

    product_norms(0)
    finish(0)
    finish(1)
    launch(0)
    launch(1)
    bias_out(0)
    product_norms(1)
    finish(2)
    finish(3)
    launch(2)
    launch(3)
    bias_out(1)
    bias_pass(0)
    relay_ring(0)
    relay_zone(0)
    product_norms(2)
    finish(4)
    finish(5)
    bias_out(2)
    launch(4)
    launch(5)
    bias_pass(1)
    relay_zone(1)
    relay_ring(1)
    bias_collect(0)
    bias_pass(2)
    bias_collect(1)
    relay_zone(2)
    relay_ring(2)
    bias_assemble(0)
    bias_assemble(1)
    relay_back(0)
    relay_zone(3)
    bias_collect(2)
    bias_assemble(2)
    relay_ring(3)
    relay_zone(4)
    relay_back(1)

    keys = table.shape[3]
    head_of_lane = lax.broadcasted_iota(jnp.int32, (columns, channels), 1) // (channels // heads)
    score_scale = LOG2E / math.sqrt(channels // heads)
    ones = jnp.ones((keys, channels), BF16)

    def attend(g, carry):
        @pl.when(g == 0)
        def _():
            relay_zone(groups - 1)
            relay_ring(groups - 2)

        @pl.when(g == 1)
        def _():
            relay_ring(groups - 1)

        for slot in (3, 4, 7):
            hop(slot, g).wait_recv()

        @pl.when(g + 2 < groups)
        def _():
            relay_back(g + 2)

        at = pl.ds(g * GROUP, GROUP)
        key_value = jnp.concatenate([key_ref[...], value_ref[...]], axis=1)
        for t in range(GROUP):
            i = g * GROUP + t
            tokens = jnp.concatenate([everything[c, i] for c in range(8)], axis=0)
            projected = dot(tokens, key_value).astype(BF16)
            key, value = projected[:, 0:channels], projected[:, channels:]
            query = dot(everything[chan, i], query_ref[...])
            split = jnp.concatenate(
                [jnp.where(head_of_lane == h, query, 0.0) for h in range(heads)], axis=0
            ).astype(BF16)
            score = dot(split, key, 1, 1) * score_scale + table[...].reshape(heads * columns, keys)
            raised = jnp.exp2(score - jnp.max(score, axis=1, keepdims=True)).astype(BF16)
            summed = dot(raised, jnp.concatenate([value, ones], axis=1))
            top = jnp.zeros((columns, channels), F32)
            bottom = jnp.ones((columns, channels), F32)
            for h in range(heads):
                mine_h = slice(h * columns, (h + 1) * columns)
                top = jnp.where(head_of_lane == h, summed[mine_h, 0:channels], top)
                bottom = jnp.where(head_of_lane == h, summed[mine_h, channels:], bottom)
            attended_f[pl.ds(t * columns, columns), :] = top / bottom

        normed = everything[chan, at].reshape(GROUP * columns, channels)
        gate = jax.nn.sigmoid(dot(normed, heads_gate_ref[...]))
        mixed = (gate * attended_f[...]).astype(BF16)
        after = after_all[at].reshape(GROUP * columns, channels).astype(F32)
        second = (after + dot(mixed, heads_out_ref[...])).astype(BF16)
        second_f = second.astype(F32)
        normed = normalize(second_f, 1).astype(BF16)
        hidden = jax.nn.silu(dot(normed, swish_ref[...])) * dot(normed, linear_ref[...])
        out = (second_f + dot(hidden.astype(BF16), project_ref[...])).astype(BF16)
        out_ref[at] = out.reshape(GROUP, columns, channels)
        return carry

    lax.fori_loop(0, groups, attend, 0)

    for part, send in enumerate((send_first, send_rest)):
        sent = send.at[pl.ds(0, 127)]
        pltpu.make_async_copy(sent, sent, edge_send.at[part]).wait()
    for phase in range(4):
        swap(phase).wait_send()
    for part in range(3):
        sent = back.at[part, pl.ds(0, 127)]
        pltpu.make_async_copy(sent, sent, back_send.at[part]).wait()
        for step in range(4):

            @pl.when(jnp.logical_not(stays((high + step) % 4)))
            def _():
                bias_copy(part, (high + step) % 4).wait_send()

        for apart in range(1, 4):
            bias_hop(part, apart).wait_send()
        for apart in range(4):
            bias_swap(part, apart).wait_send()

    def gather_wait(g, carry):
        for slot in range(8):
            hop(slot, g).wait_send()
        return carry

    lax.fori_loop(0, groups, gather_wait, 0)


def body(
    pair_input,
    token_valid,
    left_proj,
    left_gate,
    right_proj,
    right_gate,
    mult_gate,
    mult_out,
    query_weight,
    key_weight,
    value_weight,
    bias_weight,
    heads_gate,
    heads_out,
    swish_in,
    linear_in,
    project_out,
):
    rows, columns, channels = pair_input.shape
    heads = bias_weight.shape[1]
    tokens = token_valid.shape[0]
    groups = rows // GROUP
    return pl.pallas_call(
        block_kernel,
        out_shape=jax.ShapeDtypeStruct((rows, columns, channels), BF16),
        in_specs=[VMEM, pl.BlockSpec(memory_space=pltpu.SMEM)] + [VMEM] * 16,
        out_specs=VMEM,
        scratch_shapes=[
            pltpu.VMEM((rows * channels, 128), F32),
            pltpu.VMEM((rows * channels, 128), F32),
            pltpu.VMEM((rows, columns, channels), BF16),
            pltpu.VMEM((128, rows, 128), BF16),
            pltpu.VMEM((128, 16, 128), BF16),
            pltpu.VMEM((4, 32, rows, 128), BF16),
            pltpu.VMEM((4, 32, 16, 128), BF16),
            pltpu.VMEM((4, 32, rows, 128), BF16),
            pltpu.VMEM((128, 1024), BF16),
            pltpu.VMEM((256, 1024), BF16),
            pltpu.VMEM((8, 128, 1024), BF16),
            pltpu.VMEM((3, 8, 16, 8, 128), BF16),
            pltpu.VMEM((3, 128, 8, 128), BF16),
            pltpu.VMEM((rows, columns, channels), F32),
            pltpu.VMEM((channels * 8, 128), F32),
            pltpu.VMEM((rows, columns, channels), BF16),
            pltpu.VMEM((8, rows, columns, channels), BF16),
            pltpu.VMEM((rows * 8, 128), F32),
            pltpu.VMEM((3, heads - 1, 8, 128), F32),
            pltpu.VMEM((3, 4, 2, 2, heads - 1, 8, 128), F32),
            pltpu.VMEM((3, 4, 2, 2, heads - 1, 8, 128), F32),
            pltpu.VMEM((heads, 4, rows, tokens), F32),
            pltpu.VMEM((GROUP * columns, channels), F32),
            pltpu.SemaphoreType.REGULAR,
            pltpu.SemaphoreType.DMA((2,)),
            pltpu.SemaphoreType.DMA((5,)),
            pltpu.SemaphoreType.DMA((4,)),
            pltpu.SemaphoreType.DMA((4,)),
            pltpu.SemaphoreType.DMA((3,)),
            pltpu.SemaphoreType.DMA((3,)),
            pltpu.SemaphoreType.DMA((8, groups)),
            pltpu.SemaphoreType.DMA((8, groups)),
            pltpu.SemaphoreType.DMA((3, 4)),
            pltpu.SemaphoreType.DMA((3, 4)),
            pltpu.SemaphoreType.DMA((3, 4)),
            pltpu.SemaphoreType.DMA((3, 4)),
        ],
        compiler_params=pltpu.CompilerParams(
            collective_id=0, has_side_effects=True, vmem_limit_bytes=LIMIT
        ),
        name="block",
    )(
        pair_input,
        token_valid,
        token_valid,
        left_proj,
        left_gate,
        right_proj,
        right_gate,
        mult_gate,
        mult_out,
        query_weight,
        key_weight,
        value_weight,
        bias_weight.T,
        heads_gate,
        heads_out,
        swish_in,
        linear_in,
        project_out,
    )


def solution(mesh):
    return jax.shard_map(
        body,
        mesh=mesh,
        in_specs=(P("row", "chan", None),) + (P(),) * 16,
        out_specs=P("row", "chan", None),
        check_vma=False,
    )
```
